256 devices in a mesh: tile: 32 (over y, x, core), rep: 8 (over z).
Axes of the slice: x: 4, y: 4, z: 8, core: 2. Of those that a mesh axis runs over, the one named last changes fastest.
Arguments:
- input_video: bfloat16 [8, 24, 256, 64, 128], P('rep', None, 'tile'), may hold values from -60 to 60
- block_clip: int32 [8, 6], P('rep'), may hold values from 0 to 2, as said below
- send_slot: int32 [8, 32, 32, 2], P('rep', 'tile'), may hold values from 0 to 48, as said below
- recv_index: int32 [8, 32, 16], P('rep', 'tile'), may hold values from 0 to 63, as said below
- tile_clip: int32 [8, 32, 16], P('rep', 'tile'), may hold values from 0 to 2, as said below
- kernel: bfloat16 [3456, 256], replicated, may hold values from -0.109375 to 0.109375
- norm_gain: float32 [256], replicated, may hold values from 0.5 to 1.5
- norm_shift: float32 [256], replicated, may hold values from -3 to 3
- upstream: bfloat16 [8, 32, 16, 256, 256], P('rep', 'tile'), may hold values from -26 to 26
Outputs:
- activation: bfloat16 [8, 32, 16, 256, 256], P('rep', 'tile')
- kernel_grad: float32 [3456, 256], P('tile')
- norm_grads: float32 [2, 256], replicated
The draws below stay inside these ranges and needn't reach their ends.
Inputs may be any that keep to these rules, and one draw needn't show every extreme that they name: block_clip never falls, starts at 0 and each of the 3 clips holds one or more whole time blocks. send_slot[r, t, w, p] is a slot of owner t that goes to worker w in position p, or 48 for none; an owner names each slot at most once; each worker gets exactly 16 tiles from all owners together; in each replica the last owner sends all 48 slots. recv_index[r, w, j] = t * 2 + p for a non-empty send_slot[r, t, w, p]; a worker's entries are distinct and cover all such entries addressed to it. tile_clip[r, w, j] is block_clip of the time block of work tile j.
All inputs are finite; a program needn't handle non-finite values.
Results may differ from the reference program's by a relative error of at most 0.0029.
Values may be sent and summed in bfloat16 or wider, within the bound.
A program may use at most 128 MiB of HBM per device.

```python
import jax
import jax.numpy as jnp
from jax import lax

C_IN = 128
C_OUT = 256
GROUPS = 32
CPG = 8
TAPS = 27
TT = 4
TH = 8
TW = 8
TBLK = 6
CLIPS = 3
WBLK = 8
WSLOTS = 16
PEER_CAP = 2
VOX = 256
FRAMES = 24
HEIGHT = 256
WIDTH = 64
N_TILE = 32
N_REP = 8


def replica_plan(key):
    peer_count = N_TILE
    slot_total = TBLK * WBLK
    per_worker = 2 * WBLK
    capacity = (slot_total + peer_count - 1) // peer_count
    key_order, key_shift, key_pick, key_clip = jax.random.split(key, 4)
    shuffled = jax.random.permutation(key_order, peer_count).astype(jnp.int32)
    first_owner = shuffled[0]
    owner_order = jnp.where(shuffled == peer_count - 1, first_owner, shuffled)
    owner_order = jnp.where(jnp.arange(peer_count) == 0, peer_count - 1, owner_order).astype(jnp.int32)
    group_total = peer_count // 4
    shifts = jax.random.randint(key_shift, (group_total, 2), 0, per_worker).astype(jnp.int32)
    leading = (jnp.arange(group_total) == 0)[:, None]
    shifts = jnp.where(leading, per_worker, shifts).astype(jnp.int32)
    steady = jnp.full((group_total,), per_worker, jnp.int32)
    group_counts = jnp.stack([per_worker + shifts[:, 0] + shifts[:, 1], per_worker - shifts[:, 0], per_worker - shifts[:, 1], steady], axis=1).reshape(-1)
    counts = jnp.zeros((peer_count,), jnp.int32).at[owner_order].set(group_counts.astype(jnp.int32))
    starts = jnp.cumsum(counts) - counts

    def shuffle_slots(slot_key):
        return jax.random.permutation(slot_key, slot_total).astype(jnp.int32)
    slot_order = jax.vmap(shuffle_slots)(jax.random.split(key_pick, peer_count))
    rank_index = jnp.arange(slot_total, dtype=jnp.int32)[None, :] * jnp.ones((peer_count, 1), jnp.int32)
    is_live = rank_index < counts[:, None]
    global_index = starts[:, None] + rank_index
    worker = global_index % peer_count
    depth_index = rank_index // peer_count
    work_slot = global_index // peer_count
    owner = jnp.arange(peer_count, dtype=jnp.int32)[:, None] * jnp.ones((1, slot_total), jnp.int32)
    drop_depth = jnp.where(is_live, depth_index, capacity)
    send_table = jnp.full((peer_count, peer_count, capacity), slot_total, jnp.int32).at[owner, worker, drop_depth].set(slot_order, mode='drop')
    drop_slot = jnp.where(is_live, work_slot, per_worker)
    recv_table = jnp.zeros((peer_count, per_worker), jnp.int32).at[worker, drop_slot].set(owner * capacity + depth_index, mode='drop')
    clip_starts = jnp.sort(jax.random.permutation(key_clip, TBLK - 1)[:CLIPS - 1].astype(jnp.int32) + 1)
    clip_table = jnp.sum((jnp.arange(TBLK, dtype=jnp.int32)[:, None] >= clip_starts[None, :]).astype(jnp.int32), axis=1)
    member_table = jnp.zeros((peer_count, per_worker), jnp.int32).at[worker, drop_slot].set(clip_table[slot_order // WBLK], mode='drop')
    destination = jnp.full((peer_count, slot_total), -1, jnp.int32).at[owner, slot_order].set(jnp.where(is_live, worker, -1))
    return (clip_table, send_table, recv_table, member_table, destination)


def plan_tables(key):
    return jax.vmap(replica_plan)(jax.random.split(key, N_REP))


def draw_block_clip(key, part):
    return plan_tables(key)[0].astype(jnp.int32)


def draw_send_slot(key, part):
    return plan_tables(key)[1].astype(jnp.int32)


def draw_recv_index(key, part):
    return plan_tables(key)[2].astype(jnp.int32)


def draw_tile_clip(key, part):
    return plan_tables(key)[3].astype(jnp.int32)


def draw_input_video(key, part):
    destination = plan_tables(key)[4]
    key = jax.random.fold_in(key, 7)
    key_base, key_rough, key_common, key_spare = jax.random.split(key, 4)
    position = destination.astype(jnp.float32) / float(max(N_TILE - 1, 1))
    full_shape = (N_REP, TBLK, TT, N_TILE, TH, WBLK, TW, C_IN)
    spare = jax.random.uniform(key_spare, destination.shape, jnp.float32)
    tile_scale = jnp.where(destination >= 0, 1.0 + 2.0 * position, 1.0 + 2.0 * spare)
    base = jnp.clip(jax.random.normal(key_base, full_shape, jnp.float32), -4.0, 4.0)
    common = 0.4 * jnp.clip(jax.random.normal(key_common, (N_REP, C_IN), jnp.float32), -4.0, 4.0)
    rough = jax.random.uniform(key_rough, full_shape, jnp.float32, 0.5, 1.5)
    scale_grid = tile_scale.reshape(N_REP, N_TILE, TBLK, WBLK).transpose(0, 2, 1, 3)
    values = (base * rough + common[:, None, None, None, None, None, None, :]) * scale_grid[:, :, None, :, None, :, None, None]
    return values.reshape(N_REP, FRAMES, HEIGHT, WIDTH, C_IN).astype(jnp.bfloat16)


def draw_upstream(key, part):
    key = jax.random.fold_in(key, 13)
    key_base, key_rough = jax.random.split(key, 2)
    full_shape = (N_REP, N_TILE, WSLOTS, VOX, C_OUT)
    position = jnp.arange(N_TILE, dtype=jnp.float32) / float(max(N_TILE - 1, 1))
    worker_scale = 1.0 + 2.0 * position
    base = jnp.clip(jax.random.normal(key_base, full_shape, jnp.float32), -4.0, 4.0)
    rough = jax.random.uniform(key_rough, full_shape, jnp.float32, 0.5, 1.5)
    values = base * rough * worker_scale[None, :, None, None, None]
    return values.astype(jnp.bfloat16)


def scatter_about(stream_key, shape, scale, bound, kind=jnp.bfloat16):
    values = scale * jax.random.normal(stream_key, shape, jnp.float32)
    return jnp.clip(values, min=-bound, max=bound).astype(kind)


def setup_inputs(seed: int = 0) -> dict:
    streams_of = jax.random.split(jax.random.key(seed), 10)
    input_video = draw_input_video(jax.random.fold_in(streams_of[9], 71), 0)
    block_clip = draw_block_clip(jax.random.fold_in(streams_of[9], 71), 0)
    send_slot = draw_send_slot(jax.random.fold_in(streams_of[9], 71), 0)
    recv_index = draw_recv_index(jax.random.fold_in(streams_of[9], 71), 0)
    tile_clip = draw_tile_clip(jax.random.fold_in(streams_of[9], 71), 0)
    kernel = scatter_about(streams_of[5], (TAPS * C_IN, C_OUT), (TAPS * C_IN) ** -0.5, 0.109375)
    norm_gain = jnp.clip(jax.random.uniform(streams_of[6], (C_OUT,), jnp.float32, 0.5, 1.5), 0.5, 1.5)
    norm_shift = scatter_about(streams_of[7], (C_OUT,), 0.5, 3.0, jnp.float32)
    upstream = draw_upstream(jax.random.fold_in(streams_of[9], 71), 0)
    return dict(input_video=input_video, block_clip=block_clip, send_slot=send_slot, recv_index=recv_index, tile_clip=tile_clip, kernel=kernel, norm_gain=norm_gain, norm_shift=norm_shift, upstream=upstream)


epsilon = 1e-05
highest = lax.Precision.HIGHEST

def cut_tile(padded, clip_ids, strip_row, slot_id):
    block_id = slot_id // WBLK
    width_block = slot_id % WBLK
    zero_start = jnp.zeros((), jnp.int32)
    section = lax.dynamic_slice(padded, (block_id * TT, strip_row, width_block * TW, zero_start), (TT + 2, TH + 2, TW + 2, C_IN))
    earlier = clip_ids[jnp.maximum(block_id - 1, 0)]
    linked = jnp.logical_and(block_id > 0, earlier == clip_ids[block_id])
    history = jnp.where(linked, section[:2], jnp.zeros_like(section[:2]))
    return jnp.concatenate([history, section[2:]], axis=0)

def unfold(tile_stack):
    columns = []
    for offset_t in range(3):
        for offset_h in range(3):
            for offset_w in range(3):
                columns.append(tile_stack[:, offset_t:offset_t + TT, offset_h:offset_h + TH, offset_w:offset_w + TW, :])
    return jnp.stack(columns, axis=4).reshape(-1, 27 * tile_stack.shape[-1])

def group_table(onehot, per_tile):
    return jnp.einsum('sk,sg->kg', onehot, per_tile, precision=highest)

def spread_table(onehot, group_values):
    return jnp.einsum('sk,kg->sg', onehot, group_values, precision=highest)

def reference(input_video, block_clip, send_slot, recv_index, tile_clip, kernel, norm_gain, norm_shift, upstream):
    loss_scale = float(N_REP * N_TILE * WSLOTS * VOX) ** (-0.5)

    def replica(inputs):
        frames, clip_ids, send_plan, wanted, members, cotangent = inputs
        padded = jnp.pad(frames, ((2, 0), (1, 1), (1, 1), (0, 0)))
        source = wanted // PEER_CAP
        position = wanted % PEER_CAP
        worker = jnp.arange(N_TILE, dtype=jnp.int32)[:, None] * jnp.ones_like(wanted)
        slot_ids = send_plan[source, worker, position]
        strip_rows = (source * TH).astype(jnp.int32)

        def tiles_of(rows_here, slots_here):

            def one_tile(strip_row, slot_id):
                return cut_tile(padded, clip_ids, strip_row, slot_id)
            return jax.vmap(one_tile)(rows_here, slots_here)

        def forward_worker(work_item):
            rows_here, slots_here = work_item
            return jnp.dot(unfold(tiles_of(rows_here, slots_here)), kernel, preferred_element_type=jnp.float32)
        outputs = lax.map(forward_worker, (strip_rows, slot_ids))
        grouped = outputs.reshape(-1, VOX, GROUPS, CPG)
        onehot = (members.reshape(-1)[:, None] == jnp.arange(CLIPS, dtype=jnp.int32)[None, :]).astype(jnp.float32)
        voxel_count = lax.optimization_barrier(jnp.sum(onehot, axis=0)) * float(VOX * CPG)
        first_sums = group_table(onehot, lax.optimization_barrier(jnp.sum(grouped, axis=(1, 3))))
        group_mean = first_sums / voxel_count[:, None]
        centred = grouped - spread_table(onehot, group_mean)[:, None, :, None]
        second = group_table(onehot, lax.optimization_barrier(jnp.sum(centred * centred, axis=(1, 3))))
        inverse_std = lax.rsqrt(second / voxel_count[:, None] + epsilon)
        tile_inverse = spread_table(onehot, inverse_std)[:, None, :, None]
        normed = (centred * tile_inverse).reshape(-1, VOX, C_OUT)
        pre_act = normed * norm_gain + norm_shift
        result = jax.nn.silu(pre_act).astype(jnp.bfloat16)
        incoming = cotangent.reshape(-1, VOX, C_OUT).astype(jnp.float32) * loss_scale
        sigmoid_act = jax.nn.sigmoid(pre_act)
        pre_grad = incoming * sigmoid_act * (1.0 + pre_act * (1.0 - sigmoid_act))
        norm_terms = jnp.stack([lax.optimization_barrier(jnp.sum(pre_grad * normed, axis=(0, 1))), lax.optimization_barrier(jnp.sum(pre_grad, axis=(0, 1)))])
        normed_grad = (pre_grad * norm_gain).reshape(-1, VOX, GROUPS, CPG)
        normed_groups = normed.reshape(-1, VOX, GROUPS, CPG)
        mean_grad = group_table(onehot, lax.optimization_barrier(jnp.sum(normed_grad, axis=(1, 3)))) / voxel_count[:, None]
        mean_cross = group_table(onehot, lax.optimization_barrier(jnp.sum(normed_grad * normed_groups, axis=(1, 3)))) / voxel_count[:, None]
        conv_grad = tile_inverse * (normed_grad - spread_table(onehot, mean_grad)[:, None, :, None] - normed_groups * spread_table(onehot, mean_cross)[:, None, :, None])
        conv_grad = conv_grad.reshape(N_TILE, WSLOTS * VOX, C_OUT).astype(jnp.bfloat16)

        def backward_worker(kernel_sum, work_item):
            rows_here, slots_here, grad_here = work_item
            patches = unfold(tiles_of(rows_here, slots_here))
            return (kernel_sum + jnp.dot(patches.T, grad_here, preferred_element_type=jnp.float32), None)
        kernel_total, unused = lax.scan(backward_worker, jnp.zeros((27 * C_IN, C_OUT), jnp.float32), (strip_rows, slot_ids, conv_grad))
        return (result.reshape(N_TILE, WSLOTS, VOX, C_OUT), kernel_total, norm_terms)
    results, kernel_parts, norm_parts = lax.map(replica, (input_video, block_clip, send_slot, recv_index, tile_clip, upstream))
    return (results, lax.optimization_barrier(jnp.sum(kernel_parts, axis=0)), lax.optimization_barrier(jnp.sum(norm_parts, axis=0)))
```

```python
from functools import partial

import jax
import jax.numpy as jnp
from jax import lax
from jax.experimental import pallas as pl
from jax.experimental.pallas import tpu as pltpu
from jax.sharding import PartitionSpec as P

C_IN = 128
C_OUT = 256
GROUPS = 32
CPG = 8
TT = 4
TH = 8
TW = 8
TBLK = 6
CLIPS = 3
WBLK = 8
WSLOTS = 16
VOX = 256


epsilon = 1e-05


MESH = pl.DeviceIdType.MESH
TAP = [(a, e, q) for a in range(3) for e in range(3) for q in range(3)]
F32, BF16 = jnp.float32, jnp.bfloat16
ROWS = 27 * C_IN
GVOX = float(VOX * CPG)
SLAB = 60 * 8
VMEM_BYTES = 60 * 1024 * 1024


def remote(src, dst, send, recv, **where):
    return pltpu.make_async_remote_copy(
        src_ref=src, dst_ref=dst, send_sem=send, recv_sem=recv, device_id=where, device_id_type=MESH
    )


def gather_block(block, buf, send, recv, me, count):
    buf[me] = block[...]

    def start(s, c):
        to = lax.rem(me + s, count)
        remote(block, buf.at[me], send.at[s], recv.at[me], tile=to).start()
        return c

    def wait(s, c):
        to = lax.rem(me + s, count)
        remote(block, buf.at[me], send.at[s], recv.at[to], tile=to).wait_send()
        remote(block, buf.at[to], send.at[s], recv.at[to], tile=to).wait_recv()
        return c

    lax.fori_loop(1, count, start, 0)
    lax.fori_loop(1, count, wait, 0)


def shifted(i, x, even, odd):
    for q in range(3):
        y = x[:, :, q : q + 8, :]
        even[q, i] = y.reshape(480, C_IN).astype(BF16)
        odd[q, i] = y[:, 1:9].reshape(384, C_IN).astype(BF16)


def tap_slab(even, odd, i, tap):
    a, e, q = tap
    out = []
    for f in range(TT):
        if e == 1:
            out.append(odd[q, i, pl.ds((f + a) * 64, 64), :])
        else:
            out.append(even[q, i, pl.ds((f + a) * 80 + e * 8, 64), :])
    return jnp.concatenate(out, axis=0)


def pair_slab(even, odd, i, p):
    left = tap_slab(even, odd, i, TAP[p])
    if p + 1 == len(TAP):
        return left
    return jnp.concatenate([left, tap_slab(even, odd, i, TAP[p + 1])], axis=1)


def main_kernel(
    n_tile, n_rep, tiles, filt, up, member, affine, act, grad, norm,
    even, odd, conv, ngrad, cgrad, sums, sq, tmean, tinv, blk, buf, half, other, part, red, zin, zout, fin, nbuf, blk2, buf2,
    g_send, g_recv, h_send, h_recv, c_send, c_recv, p_send, p_recv, z_send, z_recv, y_send, y_recv, f_send, f_recv, n_send, n_recv,
):
    me = lax.axis_index("tile")
    rep = lax.axis_index("rep")
    core = lax.rem(me, 2)
    chip = lax.div(me, 2)
    chips = n_tile // 2
    mate = chip * 2 + 1 - core
    loss_scale = float(n_rep * n_tile * WSLOTS * VOX) ** (-0.5)

    barrier = pltpu.get_barrier_semaphore()

    def greet_tile(s, c):
        pl.semaphore_signal(barrier, inc=1, device_id={"tile": lax.rem(me + s, n_tile)}, device_id_type=MESH)
        return c

    def greet_rep(s, c):
        pl.semaphore_signal(barrier, inc=1, device_id={"rep": lax.rem(rep + s, n_rep)}, device_id_type=MESH)
        return c

    lax.fori_loop(1, n_tile, greet_tile, 0)
    lax.fori_loop(1, n_rep, greet_rep, 0)

    gi = lax.broadcasted_iota(jnp.int32, (C_OUT, C_OUT), 0) >> 3
    gj = lax.broadcasted_iota(jnp.int32, (C_OUT, C_OUT), 1) >> 3
    same_group = (gi == gj).astype(F32)

    def per_group(v):
        return jnp.dot(v, same_group, precision=lax.Precision.HIGHEST, preferred_element_type=F32)

    def forward(n, c):
        for j in range(4):
            shifted(n * 4 + j, tiles[n * 4 + j].astype(F32), even, odd)
        acc = None
        for p in range(0, 27, 2):
            rows = jnp.concatenate([pair_slab(even, odd, n * 4 + j, p) for j in range(4)], axis=0)
            d = jnp.dot(rows, filt[p * C_IN : min(p + 2, 27) * C_IN, :], preferred_element_type=F32)
            acc = d if acc is None else acc + d
        for j in range(4):
            one = acc[j * VOX : (j + 1) * VOX]
            conv[n * 4 + j] = one
            sums[pl.ds(n * 4 + j, 1), :] = jnp.sum(one, axis=0, keepdims=True)
        return c

    lax.fori_loop(0, WSLOTS // 4, forward, 0)

    gsum = per_group(sums[...])
    tmean[...] = gsum / GVOX

    def centre(i, c):
        d = conv[i] - tmean[pl.ds(i, 1), :]
        sq[pl.ds(i, 1), :] = jnp.sum(d * d, axis=0, keepdims=True)
        return c

    lax.fori_loop(0, WSLOTS, centre, 0)
    gsq = per_group(sq[...])
    counts, firsts, seconds = [], [], []
    for k in range(CLIPS):
        m = member[k]
        n_k = jnp.sum(m, axis=0, keepdims=True)
        s_k = jnp.sum(m * gsum, axis=0, keepdims=True)
        mu = s_k / (GVOX * jnp.maximum(n_k, 1.0))
        off = tmean[...] - mu
        counts.append(n_k)
        firsts.append(s_k)
        seconds.append(jnp.sum(m * (gsq + GVOX * off * off), axis=0, keepdims=True))
    blk[...] = jnp.concatenate(counts + firsts + seconds + [jnp.zeros((7, C_OUT), F32)], axis=0)

    pl.semaphore_wait(barrier, n_tile + n_rep - 2)
    gather_block(blk, buf, g_send, g_recv, me, n_tile)

    all_n = buf[:, 0:3, :]
    all_s = buf[:, 3:6, :]
    n_tot = jnp.sum(all_n, axis=0)
    mean = jnp.sum(all_s, axis=0) / (GVOX * n_tot)
    off = all_s / (GVOX * jnp.maximum(all_n, 1.0)) - mean
    var = jnp.sum(buf[:, 6:9, :] + GVOX * all_n * off * off, axis=0) / (GVOX * n_tot)
    inv = lax.rsqrt(var + epsilon)
    tmean[...] = sum(member[k] * mean[k : k + 1] for k in range(CLIPS))
    tinv[...] = sum(member[k] * inv[k : k + 1] for k in range(CLIPS))

    gain = affine[0:1, :]
    shift = affine[1:2, :]

    def middle(i, c):
        mu = tmean[pl.ds(i, 1), :]
        iv = tinv[pl.ds(i, 1), :]
        first = jnp.zeros((1, C_OUT), F32)
        cross = jnp.zeros((1, C_OUT), F32)
        for r in range(0, VOX, 64):
            normed = (conv[i, r : r + 64, :] - mu) * iv
            pre = normed * gain + shift
            sg = 1.0 / (1.0 + jnp.exp(-pre))
            act[i, r : r + 64, :] = (pre * sg).astype(BF16)
            pg = (up[i, r : r + 64, :].astype(F32) * loss_scale) * sg * (1.0 + pre * (1.0 - sg))
            first += jnp.sum(pg, axis=0, keepdims=True)
            cross += jnp.sum(pg * normed, axis=0, keepdims=True)
            conv[i, r : r + 64, :] = normed
            ngrad[i, r : r + 64, :] = pg * gain
        sums[pl.ds(i, 1), :] = first
        sq[pl.ds(i, 1), :] = cross
        return c

    lax.fori_loop(0, WSLOTS, middle, 0)
    firsts = [jnp.sum(member[k] * sums[...], axis=0, keepdims=True) for k in range(CLIPS)]
    crosses = [jnp.sum(member[k] * sq[...], axis=0, keepdims=True) for k in range(CLIPS)]
    blk2[...] = jnp.concatenate(firsts + crosses + [jnp.zeros((2, C_OUT), F32)], axis=0)
    gather_block(blk2, buf2, h_send, h_recv, me, n_tile)
    total = jnp.sum(buf2[...], axis=0)

    both = jnp.concatenate(
        [jnp.sum(total[3:6], axis=0, keepdims=True), jnp.sum(total[0:3], axis=0, keepdims=True), jnp.zeros((6, C_OUT), F32)], axis=0
    )
    nbuf[rep] = both

    def norm_start(s, c):
        to = lax.rem(rep + s, n_rep)
        remote(nbuf.at[rep], nbuf.at[rep], n_send.at[s], n_recv.at[rep], rep=to).start()
        return c

    def norm_wait(s, c):
        to = lax.rem(rep + s, n_rep)
        remote(nbuf.at[rep], nbuf.at[rep], n_send.at[s], n_recv.at[to], rep=to).wait_send()
        remote(nbuf.at[rep], nbuf.at[to], n_send.at[s], n_recv.at[to], rep=to).wait_recv()
        return c

    lax.fori_loop(1, n_rep, norm_start, 0)

    scaled = per_group(total * gain)
    spread_n = GVOX * n_tot
    mg = scaled[0:3] / spread_n
    mc = scaled[3:6] / spread_n
    sums[...] = sum(member[k] * mg[k : k + 1] for k in range(CLIPS))
    sq[...] = sum(member[k] * mc[k : k + 1] for k in range(CLIPS))

    def conv_gradient(i, c):
        iv = tinv[pl.ds(i, 1), :]
        m1 = sums[pl.ds(i, 1), :]
        m2 = sq[pl.ds(i, 1), :]
        for r in range(0, VOX, 64):
            g = iv * (ngrad[i, r : r + 64, :] - m1 - conv[i, r : r + 64, :] * m2)
            cgrad[i, r : r + 64, :] = g.astype(BF16)
        return c

    lax.fori_loop(0, WSLOTS, conv_gradient, 0)

    share = ROWS // chips

    def mate_copy(p):
        rows = pl.ds(p * C_IN, (min(p + 2, 27) - p) * C_IN)
        return remote(half.at[1 - core, rows], other.at[rows], c_send.at[p // 2], c_recv.at[p // 2], tile=mate)

    def chip_copy(j, k):
        return remote(half.at[core, pl.ds(j * share, share)], part.at[k], p_send.at[j], p_recv.at[k], tile=j * 2 + core)

    done = [0]

    def settle(p):
        lo, hi = p * C_IN, min(p + 2, 27) * C_IN
        mate_copy(p).wait_recv()
        half[core, lo:hi, :] = half[core, lo:hi, :] + other[lo:hi, :]
        while (done[0] + 1) * share <= hi:
            j = done[0]

            @pl.when(chip != j)
            def _():
                chip_copy(j, chip).start()

            @pl.when(chip == j)
            def _():
                part[j] = half[core, j * share : (j + 1) * share, :]

            done[0] += 1

    lag = 4
    for p in range(0, 27, 2):
        d = None
        for u in range(0, WSLOTS, 4):
            rows = jnp.concatenate([pair_slab(even, odd, i, p) for i in range(u, u + 4)], axis=0)
            g = jnp.concatenate([cgrad[i] for i in range(u, u + 4)], axis=0)
            t = lax.dot_general(rows, g, (((0,), (0,)), ((), ())), preferred_element_type=F32)
            d = t if d is None else d + t
        lo, hi = p * C_IN, min(p + 2, 27) * C_IN
        half[0, lo:hi, :] = d[:, :128]
        half[1, lo:hi, :] = d[:, 128:]
        mate_copy(p).start()
        if p >= lag:
            settle(p - lag)
    for p in range(0, 27, 2):
        if p + lag >= 27:
            settle(p)

    def plane_wait(s, c):
        j = lax.rem(chip + s, chips)
        chip_copy(j, chip).wait_send()
        chip_copy(j, j).wait_recv()
        return c

    lax.fori_loop(1, chips, plane_wait, 0)
    for p in range(0, 27, 2):
        mate_copy(p).wait_send()

    piece = red.shape[0] // n_rep
    red[0:share, :] = jnp.sum(part[...], axis=0)
    if red.shape[0] > share:
        red[share:, :] = jnp.zeros((red.shape[0] - share, 128), F32)
    zin[rep] = red[pl.ds(pl.multiple_of(rep * piece, 8), piece), :]

    def z_copy(to, slot, s):
        return remote(red.at[pl.ds(pl.multiple_of(to * piece, 8), piece)], zin.at[slot], z_send.at[s], z_recv.at[slot], rep=to)

    def y_copy(to, slot, s):
        rows = pl.ds(pl.multiple_of(slot * piece, 8), piece)
        mine = pl.ds(pl.multiple_of(rep * piece, 8), piece)
        return remote(zout.at[mine], zout.at[rows], y_send.at[s], y_recv.at[slot], rep=to)

    def each(what):
        def body(s, c):
            what(lax.rem(rep + s, n_rep), s)
            return c

        lax.fori_loop(1, n_rep, body, 0)

    each(lambda to, s: z_copy(to, rep, s).start())
    lax.fori_loop(1, n_rep, norm_wait, 0)
    norm[...] = jnp.sum(nbuf[...], axis=0)
    each(lambda to, s: z_copy(to, rep, s).wait_send())
    each(lambda to, s: z_copy(to, to, s).wait_recv())
    zout[pl.ds(pl.multiple_of(rep * piece, 8), piece), :] = jnp.sum(zin[...], axis=0)
    each(lambda to, s: y_copy(to, rep, s).start())
    each(lambda to, s: y_copy(to, rep, s).wait_send())
    each(lambda to, s: y_copy(to, to, s).wait_recv())

    keep = grad.shape[0]
    skip = share - keep

    def rows_of(c):
        return pl.ds(pl.multiple_of(c * skip, 8), keep)

    swap = remote(zout.at[rows_of(1 - core)], fin, f_send, f_recv, tile=mate)
    swap.start()
    swap.wait()
    own = zout[rows_of(core), :]
    there = fin[...]
    grad[:, 0:128] = jnp.where(core == 0, own, there)
    grad[:, 128:256] = jnp.where(core == 0, there, own)


def main_call(n_tile, n_rep, tiles, filt, up, member, affine):
    chips = n_tile // 2
    share = ROWS // chips
    keep = share // 2 + 4 if (share // 2) % 8 else share // 2
    padded = -(-share // (8 * n_rep)) * 8 * n_rep
    whole = pl.BlockSpec(memory_space=pltpu.VMEM)
    dma = pltpu.SemaphoreType.DMA
    return pl.pallas_call(
        partial(main_kernel, n_tile, n_rep),
        out_shape=(
            jax.ShapeDtypeStruct((WSLOTS, VOX, C_OUT), BF16),
            jax.ShapeDtypeStruct((keep, C_OUT), F32),
            jax.ShapeDtypeStruct((8, C_OUT), F32),
        ),
        in_specs=[whole] * 5,
        out_specs=(whole,) * 3,
        scratch_shapes=[
            pltpu.VMEM((3, WSLOTS, 480, C_IN), BF16),
            pltpu.VMEM((3, WSLOTS, 384, C_IN), BF16),
            pltpu.VMEM((WSLOTS, VOX, C_OUT), F32),
            pltpu.VMEM((WSLOTS, VOX, C_OUT), F32),
            pltpu.VMEM((WSLOTS, VOX, C_OUT), BF16),
            pltpu.VMEM((WSLOTS, C_OUT), F32),
            pltpu.VMEM((WSLOTS, C_OUT), F32),
            pltpu.VMEM((WSLOTS, C_OUT), F32),
            pltpu.VMEM((WSLOTS, C_OUT), F32),
            pltpu.VMEM((16, C_OUT), F32),
            pltpu.VMEM((n_tile, 16, C_OUT), F32),
            pltpu.VMEM((2, ROWS, 128), F32),
            pltpu.VMEM((ROWS, 128), F32),
            pltpu.VMEM((chips, share, 128), F32),
            pltpu.VMEM((padded, 128), F32),
            pltpu.VMEM((n_rep, padded // n_rep, 128), F32),
            pltpu.VMEM((padded, 128), F32),
            pltpu.VMEM((keep, 128), F32),
            pltpu.VMEM((n_rep, 8, C_OUT), F32),
            pltpu.VMEM((8, C_OUT), F32),
            pltpu.VMEM((n_tile, 8, C_OUT), F32),
        ]
        + [dma((n_tile,))] * 4
        + [dma((14,))] * 2
        + [dma((chips,))] * 2
        + [dma((n_rep,))] * 4
        + [dma] * 2
        + [dma((n_rep,))] * 2,
        compiler_params=pltpu.CompilerParams(collective_id=0, has_side_effects=True, vmem_limit_bytes=VMEM_BYTES),
        cost_estimate=pl.CostEstimate(flops=4 * WSLOTS * VOX * ROWS * C_OUT, bytes_accessed=16 * 1024 * 1024, transcendentals=WSLOTS * VOX * C_OUT),
        name="conv_norm",
    )(tiles, filt, up, member, affine)


def extended(cells, sides, width):
    for axis, dim in sides:
        count = lax.axis_size(axis)
        ends = count - 1
        head = lax.slice_in_dim(cells, 0, width, axis=dim)
        tail = lax.slice_in_dim(cells, cells.shape[dim] - width, cells.shape[dim], axis=dim)
        cells = jnp.concatenate(
            [
                lax.ppermute(tail, axis, [(i, (i + 1) % count) for i in range(ends)]),
                cells,
                lax.ppermute(head, axis, [((i + 1) % count, i) for i in range(ends)]),
            ],
            axis=dim,
        )
    return cells


def cut_tile(padded, clip_ids, strip_row, slot_id):
    block_id = slot_id // WBLK
    width_block = slot_id % WBLK
    zero_start = jnp.zeros((), jnp.int32)
    section = lax.dynamic_slice(
        padded,
        (block_id * TT, strip_row, width_block * TW, zero_start),
        (TT + 2, TH + 2, TW + 2, C_IN),
    )
    earlier = clip_ids[jnp.maximum(block_id - 1, 0)]
    linked = jnp.logical_and(block_id > 0, earlier == clip_ids[block_id])
    history = jnp.where(linked, section[:2], jnp.zeros_like(section[:2]))
    return jnp.concatenate([history, section[2:]], axis=0)


def shards(
    input_video,
    block_clip,
    send_slot,
    recv_index,
    tile_clip,
    kernel,
    norm_gain,
    norm_shift,
    upstream,
):
    peer_count = lax.axis_size("tile")
    frames = input_video[0]
    clip_ids = block_clip[0]
    rimmed = extended(frames, (("tile", 1),), 1)
    padded = jnp.pad(rimmed, ((2, 0), (0, 0), (1, 1), (0, 0)))
    send_plan = send_slot[0, 0]
    capacity = send_plan.shape[1]
    chosen = jnp.minimum(send_plan.reshape(-1), TBLK * WBLK - 1)
    zero_rows = jnp.zeros_like(chosen)
    outgoing = jax.vmap(partial(cut_tile, padded, clip_ids))(zero_rows, chosen)
    outgoing = outgoing.reshape((peer_count, capacity) + outgoing.shape[1:])
    arrived = lax.all_to_all(outgoing, "tile", split_axis=0, concat_axis=0, tiled=True)
    arrived = arrived.reshape((peer_count * capacity,) + arrived.shape[2:])
    work_tiles = arrived[recv_index[0, 0]]

    clips = jnp.arange(CLIPS, dtype=jnp.int32)[:, None, None]
    member = jnp.broadcast_to((tile_clip[0, 0][None, :, None] == clips).astype(F32), (CLIPS, WSLOTS, C_OUT))
    affine = jnp.concatenate([norm_gain[None], norm_shift[None], jnp.zeros((6, C_OUT), F32)], axis=0)
    activation, grad_rows, norm_rows = main_call(
        peer_count, lax.axis_size("rep"), work_tiles, kernel, upstream[0, 0], member, affine
    )
    row_share = ROWS // peer_count
    skip = (grad_rows.shape[0] - row_share) * lax.rem(lax.axis_index("tile"), 2)
    grad_shard = lax.dynamic_slice_in_dim(grad_rows, skip, row_share, 0)
    return (activation[None, None], grad_shard, norm_rows[:2])


def solution(mesh):
    placed = (
        P("rep", None, "tile", None, None),
        P("rep", None),
        P("rep", "tile", None, None),
        P("rep", "tile", None),
        P("rep", "tile", None),
        P(),
        P(),
        P(),
        P("rep", "tile", None, None, None),
    )
    return jax.shard_map(
        shards,
        mesh=mesh,
        in_specs=placed,
        out_specs=(P("rep", "tile", None, None, None), P("tile", None), P()),
        check_vma=False,
    )
```

```python
from functools import partial

import jax
import jax.numpy as jnp
from jax import lax
from jax.experimental import pallas as pl
from jax.experimental.pallas import tpu as pltpu
from jax.sharding import PartitionSpec as P

C_IN = 128
C_OUT = 256
GROUPS = 32
CPG = 8
TT = 4
TH = 8
TW = 8
TBLK = 6
CLIPS = 3
WBLK = 8
WSLOTS = 16
VOX = 256
FRAMES = 24


epsilon = 1e-05


MESH = pl.DeviceIdType.MESH
TAP = [(a, e, q) for a in range(3) for e in range(3) for q in range(3)]
F32, BF16 = jnp.float32, jnp.bfloat16
ROWS = 27 * C_IN
GVOX = float(VOX * CPG)
SLAB = 60 * 8
VMEM_BYTES = 60 * 1024 * 1024


def remote(src, dst, send, recv, **where):
    return pltpu.make_async_remote_copy(
        src_ref=src, dst_ref=dst, send_sem=send, recv_sem=recv, device_id=where, device_id_type=MESH
    )


def gather_block(block, buf, send, recv, me, count):
    buf[me] = block[...]

    def start(s, c):
        to = lax.rem(me + s, count)
        remote(block, buf.at[me], send.at[s], recv.at[me], tile=to).start()
        return c

    def wait(s, c):
        to = lax.rem(me + s, count)
        remote(block, buf.at[me], send.at[s], recv.at[to], tile=to).wait_send()
        remote(block, buf.at[to], send.at[s], recv.at[to], tile=to).wait_recv()
        return c

    lax.fori_loop(1, count, start, 0)
    lax.fori_loop(1, count, wait, 0)


def shifted(i, x, even, odd):
    for q in range(3):
        y = x[:, :, q : q + 8, :]
        even[q, i] = y.reshape(480, C_IN).astype(BF16)
        odd[q, i] = y[:, 1:9].reshape(384, C_IN).astype(BF16)


def tap_slab(even, odd, i, tap):
    a, e, q = tap
    out = []
    for f in range(TT):
        if e == 1:
            out.append(odd[q, i, pl.ds((f + a) * 64, 64), :])
        else:
            out.append(even[q, i, pl.ds((f + a) * 80 + e * 8, 64), :])
    return jnp.concatenate(out, axis=0)


def pair_slab(even, odd, i, p):
    left = tap_slab(even, odd, i, TAP[p])
    if p + 1 == len(TAP):
        return left
    return jnp.concatenate([left, tap_slab(even, odd, i, TAP[p + 1])], axis=1)


def main_kernel(
    n_tile, n_rep, tiles, filt, up, member, affine, act, grad, norm,
    even, odd, conv, ngrad, cgrad, sums, sq, tmean, tinv, blk, buf, half, other, part, red, zin, zout, fin, nbuf, blk2, buf2,
    g_send, g_recv, h_send, h_recv, c_send, c_recv, p_send, p_recv, z_send, z_recv, y_send, y_recv, f_send, f_recv, n_send, n_recv,
):
    me = lax.axis_index("tile")
    rep = lax.axis_index("rep")
    core = lax.rem(me, 2)
    chip = lax.div(me, 2)
    chips = n_tile // 2
    mate = chip * 2 + 1 - core
    loss_scale = float(n_rep * n_tile * WSLOTS * VOX) ** (-0.5)

    barrier = pltpu.get_barrier_semaphore()

    def greet_tile(s, c):
        pl.semaphore_signal(barrier, inc=1, device_id={"tile": lax.rem(me + s, n_tile)}, device_id_type=MESH)
        return c

    def greet_rep(s, c):
        pl.semaphore_signal(barrier, inc=1, device_id={"rep": lax.rem(rep + s, n_rep)}, device_id_type=MESH)
        return c

    lax.fori_loop(1, n_tile, greet_tile, 0)
    lax.fori_loop(1, n_rep, greet_rep, 0)

    gi = lax.broadcasted_iota(jnp.int32, (C_OUT, C_OUT), 0) >> 3
    gj = lax.broadcasted_iota(jnp.int32, (C_OUT, C_OUT), 1) >> 3
    same_group = (gi == gj).astype(F32)

    def per_group(v):
        return jnp.dot(v, same_group, precision=lax.Precision.HIGHEST, preferred_element_type=F32)

    def forward(n, c):
        for j in range(4):
            shifted(n * 4 + j, tiles[n * 4 + j].astype(F32), even, odd)
        acc = None
        for p in range(0, 27, 2):
            rows = jnp.concatenate([pair_slab(even, odd, n * 4 + j, p) for j in range(4)], axis=0)
            d = jnp.dot(rows, filt[p * C_IN : min(p + 2, 27) * C_IN, :], preferred_element_type=F32)
            acc = d if acc is None else acc + d
        for j in range(4):
            one = acc[j * VOX : (j + 1) * VOX]
            conv[n * 4 + j] = one
            sums[pl.ds(n * 4 + j, 1), :] = jnp.sum(one, axis=0, keepdims=True)
        return c

    lax.fori_loop(0, WSLOTS // 4, forward, 0)

    gsum = per_group(sums[...])
    tmean[...] = gsum / GVOX

    def centre(i, c):
        d = conv[i] - tmean[pl.ds(i, 1), :]
        sq[pl.ds(i, 1), :] = jnp.sum(d * d, axis=0, keepdims=True)
        return c

    lax.fori_loop(0, WSLOTS, centre, 0)
    gsq = per_group(sq[...])
    counts, firsts, seconds = [], [], []
    for k in range(CLIPS):
        m = member[k]
        n_k = jnp.sum(m, axis=0, keepdims=True)
        s_k = jnp.sum(m * gsum, axis=0, keepdims=True)
        mu = s_k / (GVOX * jnp.maximum(n_k, 1.0))
        off = tmean[...] - mu
        counts.append(n_k)
        firsts.append(s_k)
        seconds.append(jnp.sum(m * (gsq + GVOX * off * off), axis=0, keepdims=True))
    blk[...] = jnp.concatenate(counts + firsts + seconds + [jnp.zeros((7, C_OUT), F32)], axis=0)

    pl.semaphore_wait(barrier, n_tile + n_rep - 2)
    gather_block(blk, buf, g_send, g_recv, me, n_tile)

    all_n = buf[:, 0:3, :]
    all_s = buf[:, 3:6, :]
    n_tot = jnp.sum(all_n, axis=0)
    mean = jnp.sum(all_s, axis=0) / (GVOX * n_tot)
    off = all_s / (GVOX * jnp.maximum(all_n, 1.0)) - mean
    var = jnp.sum(buf[:, 6:9, :] + GVOX * all_n * off * off, axis=0) / (GVOX * n_tot)
    inv = lax.rsqrt(var + epsilon)
    tmean[...] = sum(member[k] * mean[k : k + 1] for k in range(CLIPS))
    tinv[...] = sum(member[k] * inv[k : k + 1] for k in range(CLIPS))

    gain = affine[0:1, :]
    shift = affine[1:2, :]

    def middle(i, c):
        mu = tmean[pl.ds(i, 1), :]
        iv = tinv[pl.ds(i, 1), :]
        first = jnp.zeros((1, C_OUT), F32)
        cross = jnp.zeros((1, C_OUT), F32)
        for r in range(0, VOX, 64):
            normed = (conv[i, r : r + 64, :] - mu) * iv
            pre = normed * gain + shift
            sg = 1.0 / (1.0 + jnp.exp(-pre))
            act[i, r : r + 64, :] = (pre * sg).astype(BF16)
            pg = (up[i, r : r + 64, :].astype(F32) * loss_scale) * sg * (1.0 + pre * (1.0 - sg))
            first += jnp.sum(pg, axis=0, keepdims=True)
            cross += jnp.sum(pg * normed, axis=0, keepdims=True)
            conv[i, r : r + 64, :] = normed
            ngrad[i, r : r + 64, :] = pg * gain
        sums[pl.ds(i, 1), :] = first
        sq[pl.ds(i, 1), :] = cross
        return c

    lax.fori_loop(0, WSLOTS, middle, 0)
    firsts = [jnp.sum(member[k] * sums[...], axis=0, keepdims=True) for k in range(CLIPS)]
    crosses = [jnp.sum(member[k] * sq[...], axis=0, keepdims=True) for k in range(CLIPS)]
    blk2[...] = jnp.concatenate(firsts + crosses + [jnp.zeros((2, C_OUT), F32)], axis=0)
    gather_block(blk2, buf2, h_send, h_recv, me, n_tile)
    total = jnp.sum(buf2[...], axis=0)

    both = jnp.concatenate(
        [jnp.sum(total[3:6], axis=0, keepdims=True), jnp.sum(total[0:3], axis=0, keepdims=True), jnp.zeros((6, C_OUT), F32)], axis=0
    )
    nbuf[rep] = both

    def norm_start(s, c):
        to = lax.rem(rep + s, n_rep)
        remote(nbuf.at[rep], nbuf.at[rep], n_send.at[s], n_recv.at[rep], rep=to).start()
        return c

    def norm_wait(s, c):
        to = lax.rem(rep + s, n_rep)
        remote(nbuf.at[rep], nbuf.at[rep], n_send.at[s], n_recv.at[to], rep=to).wait_send()
        remote(nbuf.at[rep], nbuf.at[to], n_send.at[s], n_recv.at[to], rep=to).wait_recv()
        return c

    lax.fori_loop(1, n_rep, norm_start, 0)

    scaled = per_group(total * gain)
    spread_n = GVOX * n_tot
    mg = scaled[0:3] / spread_n
    mc = scaled[3:6] / spread_n
    sums[...] = sum(member[k] * mg[k : k + 1] for k in range(CLIPS))
    sq[...] = sum(member[k] * mc[k : k + 1] for k in range(CLIPS))

    def conv_gradient(i, c):
        iv = tinv[pl.ds(i, 1), :]
        m1 = sums[pl.ds(i, 1), :]
        m2 = sq[pl.ds(i, 1), :]
        for r in range(0, VOX, 64):
            g = iv * (ngrad[i, r : r + 64, :] - m1 - conv[i, r : r + 64, :] * m2)
            cgrad[i, r : r + 64, :] = g.astype(BF16)
        return c

    lax.fori_loop(0, WSLOTS, conv_gradient, 0)

    share = ROWS // chips

    def mate_copy(p):
        rows = pl.ds(p * C_IN, (min(p + 2, 27) - p) * C_IN)
        return remote(half.at[1 - core, rows], other.at[rows], c_send.at[p // 2], c_recv.at[p // 2], tile=mate)

    def chip_copy(j, k):
        return remote(half.at[core, pl.ds(j * share, share)], part.at[k], p_send.at[j], p_recv.at[k], tile=j * 2 + core)

    done = [0]

    def settle(p):
        lo, hi = p * C_IN, min(p + 2, 27) * C_IN
        mate_copy(p).wait_recv()
        half[core, lo:hi, :] = half[core, lo:hi, :] + other[lo:hi, :]
        while (done[0] + 1) * share <= hi:
            j = done[0]

            @pl.when(chip != j)
            def _():
                chip_copy(j, chip).start()

            @pl.when(chip == j)
            def _():
                part[j] = half[core, j * share : (j + 1) * share, :]

            done[0] += 1

    lag = 4
    for p in range(0, 27, 2):
        d = None
        for u in range(0, WSLOTS, 4):
            rows = jnp.concatenate([pair_slab(even, odd, i, p) for i in range(u, u + 4)], axis=0)
            g = jnp.concatenate([cgrad[i] for i in range(u, u + 4)], axis=0)
            t = lax.dot_general(rows, g, (((0,), (0,)), ((), ())), preferred_element_type=F32)
            d = t if d is None else d + t
        lo, hi = p * C_IN, min(p + 2, 27) * C_IN
        half[0, lo:hi, :] = d[:, :128]
        half[1, lo:hi, :] = d[:, 128:]
        mate_copy(p).start()
        if p >= lag:
            settle(p - lag)
    for p in range(0, 27, 2):
        if p + lag >= 27:
            settle(p)

    def plane_wait(s, c):
        j = lax.rem(chip + s, chips)
        chip_copy(j, chip).wait_send()
        chip_copy(j, j).wait_recv()
        return c

    lax.fori_loop(1, chips, plane_wait, 0)
    for p in range(0, 27, 2):
        mate_copy(p).wait_send()

    piece = red.shape[0] // n_rep
    red[0:share, :] = jnp.sum(part[...], axis=0)
    if red.shape[0] > share:
        red[share:, :] = jnp.zeros((red.shape[0] - share, 128), F32)
    zin[rep] = red[pl.ds(pl.multiple_of(rep * piece, 8), piece), :]

    def z_copy(to, slot, s):
        return remote(red.at[pl.ds(pl.multiple_of(to * piece, 8), piece)], zin.at[slot], z_send.at[s], z_recv.at[slot], rep=to)

    def y_copy(to, slot, s):
        rows = pl.ds(pl.multiple_of(slot * piece, 8), piece)
        mine = pl.ds(pl.multiple_of(rep * piece, 8), piece)
        return remote(zout.at[mine], zout.at[rows], y_send.at[s], y_recv.at[slot], rep=to)

    def each(what):
        def body(s, c):
            what(lax.rem(rep + s, n_rep), s)
            return c

        lax.fori_loop(1, n_rep, body, 0)

    each(lambda to, s: z_copy(to, rep, s).start())
    lax.fori_loop(1, n_rep, norm_wait, 0)
    norm[...] = jnp.sum(nbuf[...], axis=0)
    each(lambda to, s: z_copy(to, rep, s).wait_send())
    each(lambda to, s: z_copy(to, to, s).wait_recv())
    zout[pl.ds(pl.multiple_of(rep * piece, 8), piece), :] = jnp.sum(zin[...], axis=0)
    each(lambda to, s: y_copy(to, rep, s).start())
    each(lambda to, s: y_copy(to, rep, s).wait_send())
    each(lambda to, s: y_copy(to, to, s).wait_recv())

    keep = grad.shape[0]
    skip = share - keep

    def rows_of(c):
        return pl.ds(pl.multiple_of(c * skip, 8), keep)

    swap = remote(zout.at[rows_of(1 - core)], fin, f_send, f_recv, tile=mate)
    swap.start()
    swap.wait()
    own = zout[rows_of(core), :]
    there = fin[...]
    grad[:, 0:128] = jnp.where(core == 0, own, there)
    grad[:, 128:256] = jnp.where(core == 0, there, own)


def main_call(n_tile, n_rep, tiles, filt, up, member, affine):
    chips = n_tile // 2
    share = ROWS // chips
    keep = share // 2 + 4 if (share // 2) % 8 else share // 2
    padded = -(-share // (8 * n_rep)) * 8 * n_rep
    whole = pl.BlockSpec(memory_space=pltpu.VMEM)
    dma = pltpu.SemaphoreType.DMA
    return pl.pallas_call(
        partial(main_kernel, n_tile, n_rep),
        out_shape=(
            jax.ShapeDtypeStruct((WSLOTS, VOX, C_OUT), BF16),
            jax.ShapeDtypeStruct((keep, C_OUT), F32),
            jax.ShapeDtypeStruct((8, C_OUT), F32),
        ),
        in_specs=[whole] * 5,
        out_specs=(whole,) * 3,
        scratch_shapes=[
            pltpu.VMEM((3, WSLOTS, 480, C_IN), BF16),
            pltpu.VMEM((3, WSLOTS, 384, C_IN), BF16),
            pltpu.VMEM((WSLOTS, VOX, C_OUT), F32),
            pltpu.VMEM((WSLOTS, VOX, C_OUT), F32),
            pltpu.VMEM((WSLOTS, VOX, C_OUT), BF16),
            pltpu.VMEM((WSLOTS, C_OUT), F32),
            pltpu.VMEM((WSLOTS, C_OUT), F32),
            pltpu.VMEM((WSLOTS, C_OUT), F32),
            pltpu.VMEM((WSLOTS, C_OUT), F32),
            pltpu.VMEM((16, C_OUT), F32),
            pltpu.VMEM((n_tile, 16, C_OUT), F32),
            pltpu.VMEM((2, ROWS, 128), F32),
            pltpu.VMEM((ROWS, 128), F32),
            pltpu.VMEM((chips, share, 128), F32),
            pltpu.VMEM((padded, 128), F32),
            pltpu.VMEM((n_rep, padded // n_rep, 128), F32),
            pltpu.VMEM((padded, 128), F32),
            pltpu.VMEM((keep, 128), F32),
            pltpu.VMEM((n_rep, 8, C_OUT), F32),
            pltpu.VMEM((8, C_OUT), F32),
            pltpu.VMEM((n_tile, 8, C_OUT), F32),
        ]
        + [dma((n_tile,))] * 4
        + [dma((14,))] * 2
        + [dma((chips,))] * 2
        + [dma((n_rep,))] * 4
        + [dma] * 2
        + [dma((n_rep,))] * 2,
        compiler_params=pltpu.CompilerParams(collective_id=0, has_side_effects=True, vmem_limit_bytes=VMEM_BYTES),
        cost_estimate=pl.CostEstimate(flops=4 * WSLOTS * VOX * ROWS * C_OUT, bytes_accessed=16 * 1024 * 1024, transcendentals=WSLOTS * VOX * C_OUT),
        name="conv_norm",
    )(tiles, filt, up, member, affine)


FMOD = 6
RMOD = 5
STOPS = FMOD * RMOD
PIECE = 20
PLANES = FRAMES // FMOD


def exchange_kernel(
    n_tile, lines, strip, mine, meta, tiles,
    tab, stab, raw, wide, stage, sendb, recvb, rows32,
    t_send, t_recv, s_sem, v_send, v_recv, v_own, w_send, w_recv,
):
    me = lax.axis_index("tile")
    my_f = lax.rem(me, FMOD)
    my_r = lax.div(me, FMOD)
    depth = lines // RMOD + 2

    barrier = pltpu.get_barrier_semaphore()

    def greet(s, c):
        pl.semaphore_signal(barrier, inc=1, device_id={"tile": lax.rem(me + s, n_tile)}, device_id_type=MESH)
        return c

    lax.fori_loop(1, n_tile, greet, 0)
    tab[me] = mine[...]
    pl.semaphore_wait(barrier, n_tile - 1)

    def table(to, slot, s):
        return remote(mine, tab.at[slot], t_send.at[s], t_recv.at[slot], tile=to)

    def table_start(s, c):
        table(lax.rem(me + s, n_tile), me, s).start()
        return c

    def table_wait(s, c):
        to = lax.rem(me + s, n_tile)
        table(to, me, s).wait_send()
        table(to, to, s).wait_recv()
        return c

    lax.fori_loop(1, n_tile, table_start, 0)

    def line(h):
        y = me * TH + h
        return lax.rem(y, RMOD) * FMOD, lax.div(y, RMOD)

    def spread(n, c):
        h = lax.div(n, FMOD)
        a = lax.rem(n + me, FMOD)
        stop, index = line(h)
        to = stop + a

        @pl.when(to != me)
        def _():
            remote(strip.at[:, a, h], raw.at[:, index], v_send.at[n], v_recv.at[index], tile=to).start()

        @pl.when(to == me)
        def _():
            pltpu.make_async_copy(strip.at[:, a, h], raw.at[:, index], v_own.at[h]).start()

        return c

    lax.fori_loop(0, TH * FMOD, spread, 0)

    def clear(i, c):
        wide[i] = jnp.zeros(wide.shape[1:], F32)
        return c

    lax.fori_loop(0, wide.shape[0], clear, 0)

    lax.fori_loop(1, n_tile, table_wait, 0)
    scalars = pltpu.make_async_copy(tab, stab, s_sem)
    scalars.start()

    @pl.when(me < STOPS)
    def _():
        def arrive(i, c):
            y = i * RMOD + my_r
            owner = lax.div(y, TH)
            h = lax.rem(y, TH)

            @pl.when(owner != me)
            def _():
                remote(strip.at[:, my_f, h], raw.at[:, i], v_send.at[0], v_recv.at[i], tile=owner).wait_recv()

            @pl.when(owner == me)
            def _():
                pltpu.make_async_copy(strip.at[:, my_f, h], raw.at[:, i], v_own.at[h]).wait()

            for k in range(PLANES):
                line = raw[k, i].astype(F32)
                gap = jnp.zeros((1, C_IN), F32)
                line = jnp.concatenate([gap, line, gap, jnp.zeros((6, C_IN), F32)], axis=0)
                wide[k * depth + i + 1] = line.reshape(WBLK + 1, 8, C_IN)
            return c

        lax.fori_loop(0, lax.div(lines - my_r + RMOD - 1, RMOD), arrive, 0)

    scalars.wait()

    @pl.when(me < STOPS)
    def _():
        def serve(s, c):
            w = lax.rem(me + s, n_tile)
            for j in range(WSLOTS):
                r = stab[w, 0, 64 + j]
                t = lax.div(r, 2)
                slot = stab[t, 0, w * 2 + lax.rem(r, 2)]
                base = meta[0, lax.div(slot, WBLK)] + meta[0, 8 + t]
                first = lax.rem(slot, WBLK)
                for half in range(2):
                    at = j * PIECE + half * 10
                    stage[at : at + 8, :] = wide[base + half, first]
                    stage[at + 8 : at + 10, :] = wide[base + half, first + 1][:2]
            sendb[w] = stage[...].astype(BF16)

            @pl.when(w != me)
            def _():
                remote(sendb.at[w], recvb.at[me], w_send.at[w], w_recv.at[me], tile=w).start()

            @pl.when(w == me)
            def _():
                recvb[me] = sendb[me]

            return c

        lax.fori_loop(1, n_tile + 1, serve, 0)

    def land(s, c):
        i = lax.rem(me + n_tile - s, n_tile)

        @pl.when(i < STOPS)
        def _():
            @pl.when(i != me)
            def _():
                remote(sendb.at[0], recvb.at[i], w_send.at[0], w_recv.at[i], tile=i).wait_recv()

            v = recvb[i].astype(F32)
            for j in range(WSLOTS):
                for half in range(2):
                    at = j * PIECE + half * 10
                    rows32[i * 2 * WSLOTS + j * 2 + half, 0:10, :] = v[at : at + 10]

        return c

    lax.fori_loop(1, n_tile + 1, land, 0)

    def build(j, c):
        r = stab[me, 0, 64 + j]
        t = lax.div(r, 2)
        b = lax.div(stab[t, 0, me * 2 + lax.rem(r, 2)], WBLK)
        for f in range(TT + 2):
            a = lax.rem(b * TT + TT + f, FMOD)
            for y in range(RMOD):
                q = lax.rem(t * TH + 4 + y, RMOD)
                at = (q * FMOD + a) * (2 * WSLOTS) + j * 2
                for half in range(2):
                    tiles[j, f, y + half * RMOD] = rows32[at + half, 0:10, :].astype(BF16)
        return c

    lax.fori_loop(0, WSLOTS, build, 0)

    def sent(n, c):
        h = lax.div(n, FMOD)
        a = lax.rem(n + me, FMOD)
        stop, index = line(h)
        to = stop + a

        @pl.when(to != me)
        def _():
            remote(strip.at[:, a, h], raw.at[:, index], v_send.at[n], v_recv.at[index], tile=to).wait_send()

        return c

    lax.fori_loop(0, TH * FMOD, sent, 0)

    @pl.when(me < STOPS)
    def _():
        def served(s, c):
            w = lax.rem(me + s, n_tile)
            remote(sendb.at[w], recvb.at[me], w_send.at[w], w_recv.at[me], tile=w).wait_send()
            return c

        lax.fori_loop(1, n_tile, served, 0)


def exchange_call(n_tile, strip, mine, meta):
    lines = n_tile * TH
    depth = lines // RMOD + 2
    whole = pl.BlockSpec(memory_space=pltpu.VMEM)
    dma = pltpu.SemaphoreType.DMA
    return pl.pallas_call(
        partial(exchange_kernel, n_tile, lines),
        out_shape=jax.ShapeDtypeStruct((WSLOTS, TT + 2, TH + 2, TW + 2, C_IN), BF16),
        in_specs=[pl.BlockSpec(memory_space=pl.ANY), whole, pl.BlockSpec(memory_space=pltpu.SMEM)],
        out_specs=whole,
        scratch_shapes=[
            pltpu.VMEM((n_tile, 1, 128), jnp.int32),
            pltpu.SMEM((n_tile, 1, 128), jnp.int32),
            pltpu.VMEM((PLANES, lines // RMOD + 1, 8 * WBLK, C_IN), BF16),
            pltpu.VMEM(((PLANES + 1) * depth, WBLK + 1, 8, C_IN), F32),
            pltpu.VMEM((WSLOTS * PIECE, C_IN), F32),
            pltpu.VMEM((n_tile, WSLOTS * PIECE, C_IN), BF16),
            pltpu.VMEM((STOPS, WSLOTS * PIECE, C_IN), BF16),
            pltpu.VMEM((STOPS * 2 * WSLOTS, 16, C_IN), F32),
            dma((n_tile,)),
            dma((n_tile,)),
            dma,
            dma((TH * FMOD,)),
            dma((lines // RMOD + 1,)),
            dma((TH,)),
            dma((n_tile,)),
            dma((STOPS,)),
        ],
        compiler_params=pltpu.CompilerParams(collective_id=1, has_side_effects=True, vmem_limit_bytes=VMEM_BYTES),
        cost_estimate=pl.CostEstimate(flops=0, bytes_accessed=16 * 1024 * 1024, transcendentals=0),
        name="exchange",
    )(strip, mine, meta)


def shards(
    input_video,
    block_clip,
    send_slot,
    recv_index,
    tile_clip,
    kernel,
    norm_gain,
    norm_shift,
    upstream,
):
    peer_count = lax.axis_size("tile")
    me = lax.axis_index("tile")
    strip = input_video[0].reshape(PLANES, FMOD, TH, 8 * WBLK, C_IN)
    clip_ids = block_clip[0]
    mine = jnp.concatenate(
        [send_slot[0, 0].reshape(-1), recv_index[0, 0], jnp.zeros((128 - 2 * peer_count - WSLOTS,), jnp.int32)]
    )[None]
    depth = peer_count * TH // RMOD + 2
    block = jnp.arange(TBLK, dtype=jnp.int32)
    place = (me % FMOD - TT * block + 2) % FMOD
    linked = jnp.concatenate([jnp.zeros((1,), bool), clip_ids[1:] == clip_ids[:-1]])
    plane = jnp.where((place >= 2) | linked, (TT * block - 2 + place) // FMOD, PLANES)
    owner = jnp.arange(peer_count, dtype=jnp.int32)
    top = owner * TH - 1
    line = (top + (me // FMOD - top) % RMOD - me // FMOD + RMOD) // RMOD
    meta = jnp.concatenate(
        [plane * depth, jnp.zeros((2,), jnp.int32), line, jnp.zeros((120 - peer_count,), jnp.int32)]
    )[None]
    work_tiles = exchange_call(peer_count, strip, mine, meta)
    clips = jnp.arange(CLIPS, dtype=jnp.int32)[:, None, None]
    member = jnp.broadcast_to((tile_clip[0, 0][None, :, None] == clips).astype(F32), (CLIPS, WSLOTS, C_OUT))
    affine = jnp.concatenate([norm_gain[None], norm_shift[None], jnp.zeros((6, C_OUT), F32)], axis=0)
    activation, grad_rows, norm_rows = main_call(
        peer_count, lax.axis_size("rep"), work_tiles, kernel, upstream[0, 0], member, affine
    )
    row_share = ROWS // peer_count
    skip = (grad_rows.shape[0] - row_share) * lax.rem(lax.axis_index("tile"), 2)
    grad_shard = lax.dynamic_slice_in_dim(grad_rows, skip, row_share, 0)
    return (activation[None, None], grad_shard, norm_rows[:2])


def solution(mesh):
    placed = (
        P("rep", None, "tile", None, None),
        P("rep", None),
        P("rep", "tile", None, None),
        P("rep", "tile", None),
        P("rep", "tile", None),
        P(),
        P(),
        P(),
        P("rep", "tile", None, None, None),
    )
    return jax.shard_map(
        shards,
        mesh=mesh,
        in_specs=placed,
        out_specs=(P("rep", "tile", None, None, None), P("tile", None), P()),
        check_vma=False,
    )
```

```python
from functools import partial

import jax
import jax.numpy as jnp
from jax import lax
from jax.experimental import pallas as pl
from jax.experimental.pallas import tpu as pltpu
from jax.sharding import PartitionSpec as P

C_IN = 128
C_OUT = 256
GROUPS = 32
CPG = 8
TT = 4
TH = 8
TW = 8
TBLK = 6
CLIPS = 3
WBLK = 8
WSLOTS = 16
VOX = 256
FRAMES = 24


epsilon = 1e-05


MESH = pl.DeviceIdType.MESH
TAP = [(a, e, q) for a in range(3) for e in range(3) for q in range(3)]
F32, BF16 = jnp.float32, jnp.bfloat16
ROWS = 27 * C_IN
SIDE = 4
GVOX = float(VOX * CPG)
SLAB = 60 * 8
VMEM_BYTES = 60 * 1024 * 1024


def remote(src, dst, send, recv, **where):
    return pltpu.make_async_remote_copy(
        src_ref=src, dst_ref=dst, send_sem=send, recv_sem=recv, device_id=where, device_id_type=MESH
    )


def gather_block(block, buf, send, recv, me, count):
    buf[me] = block[...]

    def start(s, c):
        to = lax.rem(me + s, count)
        remote(block, buf.at[me], send.at[s], recv.at[me], tile=to).start()
        return c

    def wait(s, c):
        to = lax.rem(me + s, count)
        remote(block, buf.at[me], send.at[s], recv.at[to], tile=to).wait_send()
        remote(block, buf.at[to], send.at[s], recv.at[to], tile=to).wait_recv()
        return c

    lax.fori_loop(1, count, start, 0)
    lax.fori_loop(1, count, wait, 0)


def shifted(i, x, even, odd):
    for q in range(3):
        y = x[:, :, q : q + 8, :]
        even[q, i] = y.reshape(480, C_IN).astype(BF16)
        odd[q, i] = y[:, 1:9].reshape(384, C_IN).astype(BF16)


def tap_slab(even, odd, i, tap):
    a, e, q = tap
    out = []
    for f in range(TT):
        if e == 1:
            out.append(odd[q, i, pl.ds((f + a) * 64, 64), :])
        else:
            out.append(even[q, i, pl.ds((f + a) * 80 + e * 8, 64), :])
    return jnp.concatenate(out, axis=0)


def pair_slab(even, odd, i, p):
    left = tap_slab(even, odd, i, TAP[p])
    if p + 1 == len(TAP):
        return left
    return jnp.concatenate([left, tap_slab(even, odd, i, TAP[p + 1])], axis=1)


def main_kernel(
    n_tile, n_rep, tiles, filt, up, member, affine, act, grad, norm,
    even, odd, conv, ngrad, cgrad, sums, sq, tmean, tinv, blk, buf, half, other, part, ring, part2, red, zin, zout, nbuf, blk2, buf2,
    g_send, g_recv, h_send, h_recv, c_send, c_recv, p_send, p_recv, r_send, r_recv, z_send, z_recv, y_send, y_recv, n_send, n_recv,
):
    me = lax.axis_index("tile")
    rep = lax.axis_index("rep")
    core = lax.rem(me, 2)
    chip = lax.div(me, 2)
    chips = n_tile // 2
    mate = chip * 2 + 1 - core
    loss_scale = float(n_rep * n_tile * WSLOTS * VOX) ** (-0.5)

    barrier = pltpu.get_barrier_semaphore()

    def greet_tile(s, c):
        pl.semaphore_signal(barrier, inc=1, device_id={"tile": lax.rem(me + s, n_tile)}, device_id_type=MESH)
        return c

    def greet_rep(s, c):
        pl.semaphore_signal(barrier, inc=1, device_id={"rep": lax.rem(rep + s, n_rep)}, device_id_type=MESH)
        return c

    def greet_mate(s, c):
        where = {"tile": mate, "rep": lax.rem(rep + s, n_rep)}
        pl.semaphore_signal(barrier, inc=1, device_id=where, device_id_type=MESH)
        return c

    lax.fori_loop(1, n_tile, greet_tile, 0)
    lax.fori_loop(1, n_rep, greet_rep, 0)
    lax.fori_loop(1, n_rep, greet_mate, 0)

    gi = lax.broadcasted_iota(jnp.int32, (C_OUT, C_OUT), 0) >> 3
    gj = lax.broadcasted_iota(jnp.int32, (C_OUT, C_OUT), 1) >> 3
    same_group = (gi == gj).astype(F32)

    def exact(v, w):
        return jnp.dot(v, w, precision=lax.Precision.HIGHEST, preferred_element_type=F32)

    def per_group(v):
        return exact(v, same_group)

    def packed(rows):
        ch = lax.broadcasted_iota(jnp.int32, (C_OUT, 128), 0) >> 3
        lane = lax.broadcasted_iota(jnp.int32, (C_OUT, 128), 1)
        return sum(exact(rows[k], (lane == ch + k * GROUPS).astype(F32)) for k in range(CLIPS))

    def unpacked(v, k):
        lane = lax.broadcasted_iota(jnp.int32, (128, C_OUT), 0)
        ch = lax.broadcasted_iota(jnp.int32, (128, C_OUT), 1) >> 3
        return exact(v, (lane == ch + k * GROUPS).astype(F32))

    def forward(n, c):
        for j in range(4):
            shifted(n * 4 + j, tiles[n * 4 + j].astype(F32), even, odd)
        acc = None
        for p in range(0, 27, 2):
            rows = jnp.concatenate([pair_slab(even, odd, n * 4 + j, p) for j in range(4)], axis=0)
            d = jnp.dot(rows, filt[p * C_IN : min(p + 2, 27) * C_IN, :], preferred_element_type=F32)
            acc = d if acc is None else acc + d
        for j in range(4):
            one = acc[j * VOX : (j + 1) * VOX]
            conv[n * 4 + j] = one
            sums[pl.ds(n * 4 + j, 1), :] = jnp.sum(one, axis=0, keepdims=True)
        return c

    lax.fori_loop(0, WSLOTS // 4, forward, 0)

    gsum = per_group(sums[...])
    tmean[...] = gsum / GVOX

    def centre(i, c):
        d = conv[i] - tmean[pl.ds(i, 1), :]
        sq[pl.ds(i, 1), :] = jnp.sum(d * d, axis=0, keepdims=True)
        return c

    lax.fori_loop(0, WSLOTS, centre, 0)
    local = []
    for k in range(CLIPS):
        m = member[k]
        n_k = jnp.sum(m, axis=0, keepdims=True)
        mu = jnp.sum(m * gsum, axis=0, keepdims=True) / (GVOX * jnp.maximum(n_k, 1.0))
        off = tmean[...] - mu
        first = jnp.sum(m * sums[...], axis=0, keepdims=True)
        second = jnp.sum(m * (sq[...] + float(VOX) * off * off), axis=0, keepdims=True)
        local.append(jnp.concatenate([n_k / float(CPG), first, second, jnp.zeros((5, C_OUT), F32)], axis=0))
    blk[...] = packed(local)

    pl.semaphore_wait(barrier, n_tile + 2 * n_rep - 3)
    gather_block(blk, buf, g_send, g_recv, me, n_tile)

    all_n = buf[:, 0:1, :]
    all_s = buf[:, 1:2, :]
    n_tot = jnp.maximum(jnp.sum(all_n, axis=0), 1.0)
    mean = jnp.sum(all_s, axis=0) / (GVOX * n_tot)
    off = all_s / (GVOX * jnp.maximum(all_n, 1.0)) - mean
    var = jnp.sum(buf[:, 2:3, :] + GVOX * all_n * off * off, axis=0) / (GVOX * n_tot)
    table = jnp.concatenate([mean, lax.rsqrt(var + epsilon), jnp.zeros((6, 128), F32)], axis=0)
    wide_table = [unpacked(table, k) for k in range(CLIPS)]
    tmean[...] = sum(member[k] * wide_table[k][0:1] for k in range(CLIPS))
    tinv[...] = sum(member[k] * wide_table[k][1:2] for k in range(CLIPS))

    gain = affine[0:1, :]
    shift = affine[1:2, :]

    def middle(i, c):
        mu = tmean[pl.ds(i, 1), :]
        iv = tinv[pl.ds(i, 1), :]
        first = jnp.zeros((1, C_OUT), F32)
        cross = jnp.zeros((1, C_OUT), F32)
        for r in range(0, VOX, 64):
            normed = (conv[i, r : r + 64, :] - mu) * iv
            pre = normed * gain + shift
            sg = 1.0 / (1.0 + jnp.exp(-pre))
            act[i, r : r + 64, :] = (pre * sg).astype(BF16)
            pg = (up[i, r : r + 64, :].astype(F32) * loss_scale) * sg * (1.0 + pre * (1.0 - sg))
            first += jnp.sum(pg, axis=0, keepdims=True)
            cross += jnp.sum(pg * normed, axis=0, keepdims=True)
            conv[i, r : r + 64, :] = normed
            ngrad[i, r : r + 64, :] = pg * gain
        sums[pl.ds(i, 1), :] = first
        sq[pl.ds(i, 1), :] = cross
        return c

    lax.fori_loop(0, WSLOTS, middle, 0)
    firsts = [jnp.sum(member[k] * sums[...], axis=0, keepdims=True) for k in range(CLIPS)]
    crosses = [jnp.sum(member[k] * sq[...], axis=0, keepdims=True) for k in range(CLIPS)]
    zeros = jnp.zeros((6, C_OUT), F32)
    scaled = packed([jnp.concatenate([firsts[k] * gain, crosses[k] * gain, zeros], axis=0) for k in range(CLIPS)])
    over_clips = [sum(crosses), sum(firsts)]
    halves = [v[:, lo : lo + 128] for v in over_clips for lo in (0, 128)]
    blk2[...] = jnp.concatenate([scaled[0:2]] + halves + [jnp.zeros((2, 128), F32)], axis=0)
    gather_block(blk2, buf2, h_send, h_recv, me, n_tile)
    total = jnp.sum(buf2[...], axis=0)

    nbuf[rep] = total

    def norm_start(s, c):
        to = lax.rem(rep + s, n_rep)
        remote(nbuf.at[rep], nbuf.at[rep], n_send.at[s], n_recv.at[rep], rep=to).start()
        return c

    def norm_wait(s, c):
        to = lax.rem(rep + s, n_rep)
        remote(nbuf.at[rep], nbuf.at[rep], n_send.at[s], n_recv.at[to], rep=to).wait_send()
        remote(nbuf.at[rep], nbuf.at[to], n_send.at[s], n_recv.at[to], rep=to).wait_recv()
        return c

    lax.fori_loop(1, n_rep, norm_start, 0)

    table = total / (GVOX * n_tot)
    wide_table = [unpacked(table, k) for k in range(CLIPS)]
    sums[...] = sum(member[k] * wide_table[k][0:1] for k in range(CLIPS))
    sq[...] = sum(member[k] * wide_table[k][1:2] for k in range(CLIPS))

    def conv_gradient(i, c):
        iv = tinv[pl.ds(i, 1), :]
        m1 = sums[pl.ds(i, 1), :]
        m2 = sq[pl.ds(i, 1), :]
        for r in range(0, VOX, 64):
            g = iv * (ngrad[i, r : r + 64, :] - m1 - conv[i, r : r + 64, :] * m2)
            cgrad[i, r : r + 64, :] = g.astype(BF16)
        return c

    lax.fori_loop(0, WSLOTS, conv_gradient, 0)

    share = ROWS // chips

    batches = [(0, 8), (8, 16), (16, 22), (22, 27)]

    def mate_copy(b):
        lo, hi = batches[b]
        rows = pl.ds(lo * C_IN, (hi - lo) * C_IN)
        return remote(half.at[1 - core, rows], other.at[rows], c_send.at[b], c_recv.at[b], tile=mate)

    row, col = lax.div(chip, SIDE), lax.rem(chip, SIDE)
    u = col + core * (row - col)
    v = row + core * (col - row)

    def chip_at(pu, pv):
        return pu * (1 + (SIDE - 1) * core) + pv * (SIDE - (SIDE - 1) * core)

    def place(j):
        return j % SIDE + core * (j // SIDE - j % SIDE), j // SIDE + core * (j % SIDE - j // SIDE)

    def ring_copy(j, slot, pu, pv):
        to = chip_at(pu, v) * 2 + core
        at = slot * SIDE + pv
        return remote(half.at[core, pl.ds(j * share, share)], part.at[at], p_send.at[j], p_recv.at[at], tile=to)

    def cross_copy(slot, pv):
        to = chip_at(u, pv) * 2 + core
        return remote(ring.at[pv], part2.at[slot], r_send.at[pv], r_recv.at[slot], tile=to)

    done = [0]

    def settle(b):
        lo, hi = batches[b][0] * C_IN, batches[b][1] * C_IN
        mate_copy(b).wait_recv()
        half[core, lo:hi, :] = half[core, lo:hi, :] + other[lo:hi, :]
        while (done[0] + 1) * share <= hi:
            j = done[0]

            pu, pv = place(j)

            @pl.when(pu != u)
            def _():
                ring_copy(j, u, pu, pv).start()

            @pl.when(pu == u)
            def _():
                part[u * SIDE + pv] = half[core, j * share : (j + 1) * share, :]

            done[0] += 1

    for b, (first_tap, end_tap) in enumerate(batches):
        for p in range(first_tap, end_tap, 2):
            d = None
            for n in range(0, WSLOTS, 4):
                rows = jnp.concatenate([pair_slab(even, odd, i, p) for i in range(n, n + 4)], axis=0)
                g = jnp.concatenate([cgrad[i] for i in range(n, n + 4)], axis=0)
                t = lax.dot_general(rows, g, (((0,), (0,)), ((), ())), preferred_element_type=F32)
                d = t if d is None else d + t
            lo, hi = p * C_IN, min(p + 2, 27) * C_IN
            half[0, lo:hi, :] = d[:, :128]
            half[1, lo:hi, :] = d[:, 128:]
        mate_copy(b).start()
        if b > 0:
            settle(b - 1)
    settle(len(batches) - 1)

    def ring_sum(s, c):
        pv = lax.rem(v + s, SIDE)
        for t in range(1, SIDE):
            pu = lax.rem(u + t, SIDE)
            ring_copy(0, pu, pu, pv).wait_recv()
        ring[pv] = sum(part[pu * SIDE + pv] for pu in range(SIDE))

        @pl.when(pv != v)
        def _():
            cross_copy(v, pv).start()

        @pl.when(pv == v)
        def _():
            part2[v] = ring[v]

        return c

    lax.fori_loop(1, SIDE + 1, ring_sum, 0)
    for j in range(chips):
        pu, pv = place(j)

        @pl.when(pu != u)
        def _():
            ring_copy(j, u, pu, pv).wait_send()

    for b in range(len(batches)):
        mate_copy(b).wait_send()

    def cross_wait(s, c):
        pv = lax.rem(v + s, SIDE)
        cross_copy(v, pv).wait_send()
        cross_copy(pv, pv).wait_recv()
        return c

    lax.fori_loop(1, SIDE, cross_wait, 0)

    piece = red.shape[0] // n_rep
    red[0:share, :] = jnp.sum(part2[...], axis=0)
    if red.shape[0] > share:
        red[share:, :] = jnp.zeros((red.shape[0] - share, 128), F32)
    zin[rep] = red[pl.ds(pl.multiple_of(rep * piece, 8), piece), :]

    def z_copy(to, slot, s):
        return remote(red.at[pl.ds(pl.multiple_of(to * piece, 8), piece)], zin.at[slot], z_send.at[s], z_recv.at[slot], rep=to)

    def rows_at(r):
        return pl.ds(pl.multiple_of(r * piece, 8), piece)

    def y_copy(side, to, slot, s):
        tile = me if side == 0 else mate
        from_core = core if side == 0 else 1 - core
        mine = zout.at[core, rows_at(rep)]
        there = zout.at[core, rows_at(rep)] if slot is None else zout.at[from_core, rows_at(slot)]
        got = core * n_rep + rep if slot is None else from_core * n_rep + slot
        return remote(mine, there, y_send.at[side * n_rep + s], y_recv.at[got], tile=tile, rep=to)

    def each(what):
        def body(s, c):
            what(lax.rem(rep + s, n_rep), s)
            return c

        lax.fori_loop(1, n_rep, body, 0)

    each(lambda to, s: z_copy(to, rep, s).start())
    lax.fori_loop(1, n_rep, norm_wait, 0)
    norm[...] = jnp.sum(nbuf[...], axis=0)
    each(lambda to, s: z_copy(to, rep, s).wait_send())
    each(lambda to, s: z_copy(to, to, s).wait_recv())
    zout[core, rows_at(rep), :] = jnp.sum(zin[...], axis=0)
    y_copy(1, rep, None, 0).start()
    for side in range(2):
        each(lambda to, s: y_copy(side, to, None, s).start())
    y_copy(1, rep, None, 0).wait_send()
    y_copy(1, rep, rep, 0).wait_recv()
    for side in range(2):
        each(lambda to, s: y_copy(side, to, None, s).wait_send())
        each(lambda to, s: y_copy(side, to, to, s).wait_recv())

    keep = grad.shape[0]
    own = pl.ds(pl.multiple_of(core * (share - keep), 8), keep)
    grad[:, 0:128] = zout[0, own, :]
    grad[:, 128:256] = zout[1, own, :]


def main_call(n_tile, n_rep, tiles, filt, up, member, affine):
    chips = n_tile // 2
    share = ROWS // chips
    keep = share // 2 + 4 if (share // 2) % 8 else share // 2
    padded = -(-share // (8 * n_rep)) * 8 * n_rep
    whole = pl.BlockSpec(memory_space=pltpu.VMEM)
    dma = pltpu.SemaphoreType.DMA
    return pl.pallas_call(
        partial(main_kernel, n_tile, n_rep),
        out_shape=(
            jax.ShapeDtypeStruct((WSLOTS, VOX, C_OUT), BF16),
            jax.ShapeDtypeStruct((keep, C_OUT), F32),
            jax.ShapeDtypeStruct((8, 128), F32),
        ),
        in_specs=[whole] * 5,
        out_specs=(whole,) * 3,
        scratch_shapes=[
            pltpu.VMEM((3, WSLOTS, 480, C_IN), BF16),
            pltpu.VMEM((3, WSLOTS, 384, C_IN), BF16),
            pltpu.VMEM((WSLOTS, VOX, C_OUT), F32),
            pltpu.VMEM((WSLOTS, VOX, C_OUT), F32),
            pltpu.VMEM((WSLOTS, VOX, C_OUT), BF16),
            pltpu.VMEM((WSLOTS, C_OUT), F32),
            pltpu.VMEM((WSLOTS, C_OUT), F32),
            pltpu.VMEM((WSLOTS, C_OUT), F32),
            pltpu.VMEM((WSLOTS, C_OUT), F32),
            pltpu.VMEM((8, 128), F32),
            pltpu.VMEM((n_tile, 8, 128), F32),
            pltpu.VMEM((2, ROWS, 128), F32),
            pltpu.VMEM((ROWS, 128), F32),
            pltpu.VMEM((chips, share, 128), F32),
            pltpu.VMEM((SIDE, share, 128), F32),
            pltpu.VMEM((SIDE, share, 128), F32),
            pltpu.VMEM((padded, 128), F32),
            pltpu.VMEM((n_rep, padded // n_rep, 128), F32),
            pltpu.VMEM((2, padded, 128), F32),
            pltpu.VMEM((n_rep, 8, 128), F32),
            pltpu.VMEM((8, 128), F32),
            pltpu.VMEM((n_tile, 8, 128), F32),
        ]
        + [dma((n_tile,))] * 4
        + [dma((14,))] * 2
        + [dma((chips,))] * 2
        + [dma((SIDE,))] * 2
        + [dma((n_rep,))] * 2
        + [dma((2 * n_rep,))] * 2
        + [dma((n_rep,))] * 2,
        compiler_params=pltpu.CompilerParams(collective_id=0, has_side_effects=True, vmem_limit_bytes=VMEM_BYTES),
        cost_estimate=pl.CostEstimate(flops=4 * WSLOTS * VOX * ROWS * C_OUT, bytes_accessed=16 * 1024 * 1024, transcendentals=WSLOTS * VOX * C_OUT),
        name="conv_norm",
    )(tiles, filt, up, member, affine)


FMOD = 6
RMOD = 5
STOPS = FMOD * RMOD
PIECE = 20
PLANES = FRAMES // FMOD


def ordered_peer(me, s):
    core, chip = lax.rem(me, 2), lax.div(me, 2)
    row, col = lax.div(chip, SIDE), lax.rem(chip, SIDE)
    n = lax.div(s, 2)
    p, q = lax.rem(n, SIDE), lax.rem(n + lax.div(n, SIDE), SIDE)
    x = lax.rem(col + p + core * (q - p), SIDE)
    y = lax.rem(row + q + core * (p - q), SIDE)
    return (y * SIDE + x) * 2 + lax.rem(core + lax.rem(s, 2), 2)


def exchange_kernel(
    n_tile, lines, strip, mine, meta, tiles,
    tab, stab, raw, wide, stage, sendb, recvb, rows32,
    t_send, t_recv, s_sem, v_send, v_recv, v_own, w_send, w_recv,
):
    me = lax.axis_index("tile")
    my_f = lax.rem(me, FMOD)
    my_r = lax.div(me, FMOD)
    depth = lines // RMOD + 2

    barrier = pltpu.get_barrier_semaphore()

    def greet(s, c):
        pl.semaphore_signal(barrier, inc=1, device_id={"tile": lax.rem(me + s, n_tile)}, device_id_type=MESH)
        return c

    lax.fori_loop(1, n_tile, greet, 0)
    tab[me] = mine[...]
    pl.semaphore_wait(barrier, n_tile - 1)

    def table(to, slot, s):
        return remote(mine, tab.at[slot], t_send.at[s], t_recv.at[slot], tile=to)

    def table_start(s, c):
        table(lax.rem(me + s, n_tile), me, s).start()
        return c

    def table_wait(s, c):
        to = lax.rem(me + s, n_tile)
        table(to, me, s).wait_send()
        table(to, to, s).wait_recv()
        return c

    lax.fori_loop(1, n_tile, table_start, 0)

    def lines_to(to, what):
        a = lax.rem(to, FMOD)
        h0 = lax.rem(lax.div(to, FMOD) + RMOD * TH - lax.rem(me * TH, RMOD), RMOD)

        @pl.when(to < STOPS)
        def _():
            what(a, h0, lax.div(me * TH + h0, RMOD))

            @pl.when(h0 < TH - RMOD)
            def _():
                what(a, h0 + RMOD, lax.div(me * TH + h0 + RMOD, RMOD))

    def line_copy(to, a, h, index):
        return remote(strip.at[:, a, h], raw.at[:, index], v_send.at[h * FMOD + a], v_recv.at[index], tile=to)

    def spread(s, c):
        to = ordered_peer(me, s)
        lines_to(to, lambda a, h, index: line_copy(to, a, h, index).start())
        return c

    def keep(a, h, index):
        pltpu.make_async_copy(strip.at[:, a, h], raw.at[:, index], v_own.at[h]).start()

    lax.fori_loop(1, n_tile, spread, 0)
    lines_to(me, keep)

    def clear(i, c):
        wide[i] = jnp.zeros(wide.shape[1:], F32)
        return c

    lax.fori_loop(0, wide.shape[0], clear, 0)

    lax.fori_loop(1, n_tile, table_wait, 0)
    scalars = pltpu.make_async_copy(tab, stab, s_sem)
    scalars.start()

    @pl.when(me < STOPS)
    def _():
        def arrive(i, c):
            y = i * RMOD + my_r
            owner = lax.div(y, TH)
            h = lax.rem(y, TH)

            @pl.when(owner != me)
            def _():
                remote(strip.at[:, my_f, h], raw.at[:, i], v_send.at[0], v_recv.at[i], tile=owner).wait_recv()

            @pl.when(owner == me)
            def _():
                pltpu.make_async_copy(strip.at[:, my_f, h], raw.at[:, i], v_own.at[h]).wait()

            for k in range(PLANES):
                line = raw[k, i].astype(F32)
                gap = jnp.zeros((1, C_IN), F32)
                line = jnp.concatenate([gap, line, gap, jnp.zeros((6, C_IN), F32)], axis=0)
                wide[k * depth + i + 1] = line.reshape(WBLK + 1, 8, C_IN)
            return c

        lax.fori_loop(0, lax.div(lines - my_r + RMOD - 1, RMOD), arrive, 0)

    scalars.wait()

    @pl.when(me < STOPS)
    def _():
        def serve(s, c):
            w = ordered_peer(me, lax.rem(s, n_tile))
            for j in range(WSLOTS):
                r = stab[w, 0, 64 + j]
                t = lax.div(r, 2)
                slot = stab[t, 0, w * 2 + lax.rem(r, 2)]
                base = meta[0, lax.div(slot, WBLK)] + meta[0, 8 + t]
                first = lax.rem(slot, WBLK)
                for half in range(2):
                    at = j * PIECE + half * 10
                    stage[at : at + 8, :] = wide[base + half, first]
                    stage[at + 8 : at + 10, :] = wide[base + half, first + 1][:2]
            sendb[w] = stage[...].astype(BF16)

            @pl.when(w != me)
            def _():
                remote(sendb.at[w], recvb.at[me], w_send.at[w], w_recv.at[me], tile=w).start()

            @pl.when(w == me)
            def _():
                recvb[me] = sendb[me]

            return c

        lax.fori_loop(1, n_tile + 1, serve, 0)

    def land(s, c):
        i = ordered_peer(me, lax.rem(s, n_tile))

        @pl.when(i < STOPS)
        def _():
            @pl.when(i != me)
            def _():
                remote(sendb.at[0], recvb.at[i], w_send.at[0], w_recv.at[i], tile=i).wait_recv()

            v = recvb[i].astype(F32)
            for j in range(WSLOTS):
                for half in range(2):
                    at = j * PIECE + half * 10
                    rows32[i * 2 * WSLOTS + j * 2 + half, 0:10, :] = v[at : at + 10]

        return c

    lax.fori_loop(1, n_tile + 1, land, 0)

    def build(j, c):
        r = stab[me, 0, 64 + j]
        t = lax.div(r, 2)
        b = lax.div(stab[t, 0, me * 2 + lax.rem(r, 2)], WBLK)
        for f in range(TT + 2):
            a = lax.rem(b * TT + TT + f, FMOD)
            for y in range(RMOD):
                q = lax.rem(t * TH + 4 + y, RMOD)
                at = (q * FMOD + a) * (2 * WSLOTS) + j * 2
                for half in range(2):
                    tiles[j, f, y + half * RMOD] = rows32[at + half, 0:10, :].astype(BF16)
        return c

    lax.fori_loop(0, WSLOTS, build, 0)

    def sent(s, c):
        to = ordered_peer(me, s)
        lines_to(to, lambda a, h, index: line_copy(to, a, h, index).wait_send())
        return c

    lax.fori_loop(1, n_tile, sent, 0)

    @pl.when(me < STOPS)
    def _():
        def served(s, c):
            w = lax.rem(me + s, n_tile)
            remote(sendb.at[w], recvb.at[me], w_send.at[w], w_recv.at[me], tile=w).wait_send()
            return c

        lax.fori_loop(1, n_tile, served, 0)


def exchange_call(n_tile, strip, mine, meta):
    lines = n_tile * TH
    depth = lines // RMOD + 2
    whole = pl.BlockSpec(memory_space=pltpu.VMEM)
    dma = pltpu.SemaphoreType.DMA
    return pl.pallas_call(
        partial(exchange_kernel, n_tile, lines),
        out_shape=jax.ShapeDtypeStruct((WSLOTS, TT + 2, TH + 2, TW + 2, C_IN), BF16),
        in_specs=[pl.BlockSpec(memory_space=pl.ANY), whole, pl.BlockSpec(memory_space=pltpu.SMEM)],
        out_specs=whole,
        scratch_shapes=[
            pltpu.VMEM((n_tile, 1, 128), jnp.int32),
            pltpu.SMEM((n_tile, 1, 128), jnp.int32),
            pltpu.VMEM((PLANES, lines // RMOD + 1, 8 * WBLK, C_IN), BF16),
            pltpu.VMEM(((PLANES + 1) * depth, WBLK + 1, 8, C_IN), F32),
            pltpu.VMEM((WSLOTS * PIECE, C_IN), F32),
            pltpu.VMEM((n_tile, WSLOTS * PIECE, C_IN), BF16),
            pltpu.VMEM((STOPS, WSLOTS * PIECE, C_IN), BF16),
            pltpu.VMEM((STOPS * 2 * WSLOTS, 16, C_IN), F32),
            dma((n_tile,)),
            dma((n_tile,)),
            dma,
            dma((TH * FMOD,)),
            dma((lines // RMOD + 1,)),
            dma((TH,)),
            dma((n_tile,)),
            dma((STOPS,)),
        ],
        compiler_params=pltpu.CompilerParams(collective_id=1, has_side_effects=True, vmem_limit_bytes=VMEM_BYTES),
        cost_estimate=pl.CostEstimate(flops=0, bytes_accessed=16 * 1024 * 1024, transcendentals=0),
        name="exchange",
    )(strip, mine, meta)


def shards(
    input_video,
    block_clip,
    send_slot,
    recv_index,
    tile_clip,
    kernel,
    norm_gain,
    norm_shift,
    upstream,
):
    peer_count = lax.axis_size("tile")
    me = lax.axis_index("tile")
    strip = input_video[0].reshape(PLANES, FMOD, TH, 8 * WBLK, C_IN)
    clip_ids = block_clip[0]
    mine = jnp.concatenate(
        [send_slot[0, 0].reshape(-1), recv_index[0, 0], jnp.zeros((128 - 2 * peer_count - WSLOTS,), jnp.int32)]
    )[None]
    depth = peer_count * TH // RMOD + 2
    block = jnp.arange(TBLK, dtype=jnp.int32)
    place = (me % FMOD - TT * block + 2) % FMOD
    linked = jnp.concatenate([jnp.zeros((1,), bool), clip_ids[1:] == clip_ids[:-1]])
    plane = jnp.where((place >= 2) | linked, (TT * block - 2 + place) // FMOD, PLANES)
    owner = jnp.arange(peer_count, dtype=jnp.int32)
    top = owner * TH - 1
    line = (top + (me // FMOD - top) % RMOD - me // FMOD + RMOD) // RMOD
    meta = jnp.concatenate(
        [plane * depth, jnp.zeros((2,), jnp.int32), line, jnp.zeros((120 - peer_count,), jnp.int32)]
    )[None]
    work_tiles = exchange_call(peer_count, strip, mine, meta)
    clips = jnp.arange(CLIPS, dtype=jnp.int32)[:, None, None]
    member = jnp.broadcast_to((tile_clip[0, 0][None, :, None] == clips).astype(F32), (CLIPS, WSLOTS, C_OUT))
    affine = jnp.concatenate([norm_gain[None], norm_shift[None], jnp.zeros((6, C_OUT), F32)], axis=0)
    activation, grad_rows, norm_rows = main_call(
        peer_count, lax.axis_size("rep"), work_tiles, kernel, upstream[0, 0], member, affine
    )
    row_share = ROWS // peer_count
    skip = (grad_rows.shape[0] - row_share) * lax.rem(lax.axis_index("tile"), 2)
    grad_shard = lax.dynamic_slice_in_dim(grad_rows, skip, row_share, 0)
    return (activation[None, None], grad_shard, norm_rows[2:6].reshape(2, C_OUT))


def solution(mesh):
    placed = (
        P("rep", None, "tile", None, None),
        P("rep", None),
        P("rep", "tile", None, None),
        P("rep", "tile", None),
        P("rep", "tile", None),
        P(),
        P(),
        P(),
        P("rep", "tile", None, None, None),
    )
    return jax.shard_map(
        shards,
        mesh=mesh,
        in_specs=placed,
        out_specs=(P("rep", "tile", None, None, None), P("tile", None), P()),
        check_vma=False,
    )
```

```python
from functools import partial

import jax
import jax.numpy as jnp
from jax import lax
from jax.experimental import pallas as pl
from jax.experimental.pallas import tpu as pltpu
from jax.sharding import PartitionSpec as P

C_IN = 128
C_OUT = 256
GROUPS = 32
CPG = 8
TT = 4
TH = 8
TW = 8
TBLK = 6
CLIPS = 3
WBLK = 8
WSLOTS = 16
VOX = 256
FRAMES = 24


epsilon = 1e-05


MESH = pl.DeviceIdType.MESH
TAP = [(a, e, q) for a in range(3) for e in range(3) for q in range(3)]
F32, BF16 = jnp.float32, jnp.bfloat16
ROWS = 27 * C_IN
SIDE = 4
GVOX = float(VOX * CPG)
SLAB = 60 * 8
VMEM_BYTES = 60 * 1024 * 1024


def remote(src, dst, send, recv, **where):
    return pltpu.make_async_remote_copy(
        src_ref=src, dst_ref=dst, send_sem=send, recv_sem=recv, device_id=where, device_id_type=MESH
    )


def gather_block(block, buf, send, recv, me, count):
    buf[me] = block[...]

    def start(s, c):
        to = lax.rem(me + s, count)
        remote(block, buf.at[me], send.at[s], recv.at[me], tile=to).start()
        return c

    def wait(s, c):
        to = lax.rem(me + s, count)
        remote(block, buf.at[me], send.at[s], recv.at[to], tile=to).wait_send()
        remote(block, buf.at[to], send.at[s], recv.at[to], tile=to).wait_recv()
        return c

    lax.fori_loop(1, count, start, 0)
    lax.fori_loop(1, count, wait, 0)


def shifted(i, x, even, odd):
    for q in range(3):
        y = x[:, :, q : q + 8, :]
        even[q, i] = y.reshape(480, C_IN).astype(BF16)
        odd[q, i] = y[:, 1:9].reshape(384, C_IN).astype(BF16)


def tap_slab(even, odd, i, tap):
    a, e, q = tap
    out = []
    for f in range(TT):
        if e == 1:
            out.append(odd[q, i, pl.ds((f + a) * 64, 64), :])
        else:
            out.append(even[q, i, pl.ds((f + a) * 80 + e * 8, 64), :])
    return jnp.concatenate(out, axis=0)


def pair_slab(even, odd, i, p):
    left = tap_slab(even, odd, i, TAP[p])
    if p + 1 == len(TAP):
        return left
    return jnp.concatenate([left, tap_slab(even, odd, i, TAP[p + 1])], axis=1)


FMOD = 6
RMOD = 5
STOPS = FMOD * RMOD
PIECE = 20
PART = WSLOTS // 2
PLANES = FRAMES // FMOD


def ordered_peer(me, s):
    core, chip = lax.rem(me, 2), lax.div(me, 2)
    row, col = lax.div(chip, SIDE), lax.rem(chip, SIDE)
    n = lax.div(s, 2)
    p, q = lax.rem(n, SIDE), lax.rem(n + lax.div(n, SIDE), SIDE)
    x = lax.rem(col + p + core * (q - p), SIDE)
    y = lax.rem(row + q + core * (p - q), SIDE)
    return (y * SIDE + x) * 2 + lax.rem(core + lax.rem(s, 2), 2)


def exchange(
    n_tile, me, greeted, strip, mine, meta,
    tab, stab, raw, wide, stage, sendb, recvb, rows32,
    t_send, t_recv, s_sem, v_send, v_recv, v_own, w_send, w_recv,
):
    lines = n_tile * TH
    my_f = lax.rem(me, FMOD)
    my_r = lax.div(me, FMOD)
    depth = lines // RMOD + 2
    tab[me] = mine[...]
    greeted()

    def table(to, slot, s):
        return remote(mine, tab.at[slot], t_send.at[s], t_recv.at[slot], tile=to)

    def table_start(s, c):
        table(lax.rem(me + s, n_tile), me, s).start()
        return c

    def table_wait(s, c):
        to = lax.rem(me + s, n_tile)
        table(to, me, s).wait_send()
        table(to, to, s).wait_recv()
        return c

    lax.fori_loop(1, n_tile, table_start, 0)

    def lines_to(to, what):
        a = lax.rem(to, FMOD)
        h0 = lax.rem(lax.div(to, FMOD) + RMOD * TH - lax.rem(me * TH, RMOD), RMOD)

        @pl.when(to < STOPS)
        def _():
            what(a, h0, lax.div(me * TH + h0, RMOD))

            @pl.when(h0 < TH - RMOD)
            def _():
                what(a, h0 + RMOD, lax.div(me * TH + h0 + RMOD, RMOD))

    def line_copy(to, a, h, index):
        return remote(strip.at[:, a, h], raw.at[:, index], v_send.at[h * FMOD + a], v_recv.at[index], tile=to)

    def spread(s, c):
        to = ordered_peer(me, s)
        lines_to(to, lambda a, h, index: line_copy(to, a, h, index).start())
        return c

    def keep(a, h, index):
        pltpu.make_async_copy(strip.at[:, a, h], raw.at[:, index], v_own.at[h]).start()

    lax.fori_loop(1, n_tile, spread, 0)
    lines_to(me, keep)

    def clear(i, c):
        wide[i] = jnp.zeros(wide.shape[1:], F32)
        return c

    lax.fori_loop(0, wide.shape[0], clear, 0)

    lax.fori_loop(1, n_tile, table_wait, 0)
    scalars = pltpu.make_async_copy(tab, stab, s_sem)
    scalars.start()

    @pl.when(me < STOPS)
    def _():
        def arrive(i, c):
            y = i * RMOD + my_r
            owner = lax.div(y, TH)
            h = lax.rem(y, TH)

            @pl.when(owner != me)
            def _():
                remote(strip.at[:, my_f, h], raw.at[:, i], v_send.at[0], v_recv.at[i], tile=owner).wait_recv()

            @pl.when(owner == me)
            def _():
                pltpu.make_async_copy(strip.at[:, my_f, h], raw.at[:, i], v_own.at[h]).wait()

            for k in range(PLANES):
                line = raw[k, i].astype(F32)
                gap = jnp.zeros((1, C_IN), F32)
                line = jnp.concatenate([gap, line, gap, jnp.zeros((6, C_IN), F32)], axis=0)
                wide[k * depth + i + 1] = line.reshape(WBLK + 1, 8, C_IN)
            return c

        lax.fori_loop(0, lax.div(lines - my_r + RMOD - 1, RMOD), arrive, 0)

    scalars.wait()

    def part_copy(w, slot, h):
        return remote(sendb.at[w * 2 + h], recvb.at[slot * 2 + h], w_send.at[w * 2 + h], w_recv.at[slot * 2 + h], tile=w)

    @pl.when(me < STOPS)
    def _():
        def serve(step, c):
            h = lax.div(step, n_tile)
            w = ordered_peer(me, lax.rem(step + 1, n_tile))
            for j in range(PART):
                r = stab[w, 0, 64 + h * PART + j]
                t = lax.div(r, 2)
                slot = stab[t, 0, w * 2 + lax.rem(r, 2)]
                base = meta[0, lax.div(slot, WBLK)] + meta[0, 8 + t]
                first = lax.rem(slot, WBLK)
                for half in range(2):
                    at = j * PIECE + half * 10
                    stage[at : at + 8, :] = wide[base + half, first]
                    stage[at + 8 : at + 10, :] = wide[base + half, first + 1][:2]
            sendb[w * 2 + h] = stage[...].astype(BF16)

            @pl.when(w != me)
            def _():
                part_copy(w, me, h).start()

            @pl.when(w == me)
            def _():
                recvb[me * 2 + h] = sendb[me * 2 + h]

            return c

        lax.fori_loop(0, 2 * n_tile, serve, 0)

    def land(h):
        def body(s, c):
            i = ordered_peer(me, lax.rem(s, n_tile))

            @pl.when(i < STOPS)
            def _():
                @pl.when(i != me)
                def _():
                    part_copy(i, i, h).wait_recv()

                v = recvb[i * 2 + h].astype(F32)
                for j in range(PART):
                    for half in range(2):
                        at = j * PIECE + half * 10
                        rows32[i * 2 * PART + j * 2 + half, 0:10, :] = v[at : at + 10]

            return c

        lax.fori_loop(1, n_tile + 1, body, 0)

    def tile_rows(h, j):
        r = stab[me, 0, 64 + h * PART + j]
        t = lax.div(r, 2)
        b = lax.div(stab[t, 0, me * 2 + lax.rem(r, 2)], WBLK)
        out = []
        for f in range(TT + 2):
            a = lax.rem(b * TT + TT + f, FMOD)
            for y in range(TH + 2):
                q = lax.rem(t * TH + 4 + y % RMOD, RMOD)
                at = (q * FMOD + a) * (2 * PART) + j * 2 + y // RMOD
                out.append(rows32[at, 0:10, :])
        return jnp.stack(out, axis=0).reshape(TT + 2, TH + 2, TW + 2, C_IN)

    def drain():
        def sent(s, c):
            to = ordered_peer(me, s)
            lines_to(to, lambda a, h, index: line_copy(to, a, h, index).wait_send())
            return c

        lax.fori_loop(1, n_tile, sent, 0)

        @pl.when(me < STOPS)
        def _():
            def served(s, c):
                w = lax.rem(me + s, n_tile)
                for h in range(2):
                    part_copy(w, me, h).wait_send()
                return c

            lax.fori_loop(1, n_tile, served, 0)

    return land, tile_rows, drain


def main_kernel(
    n_tile, n_rep, strip, mine, meta, filt, up, member, affine, act, grad, norm,
    even, odd, conv, ngrad, cgrad, sums, sq, tmean, tinv, blk, buf, half, other, part, ring, part2, red, zin, zout, nbuf, blk2, buf2,
    g_send, g_recv, h_send, h_recv, c_send, c_recv, p_send, p_recv, r_send, r_recv, z_send, z_recv, y_send, y_recv, n_send, n_recv, *moving,
):
    me = lax.axis_index("tile")
    rep = lax.axis_index("rep")
    core = lax.rem(me, 2)
    chip = lax.div(me, 2)
    chips = n_tile // 2
    mate = chip * 2 + 1 - core
    loss_scale = float(n_rep * n_tile * WSLOTS * VOX) ** (-0.5)

    barrier = pltpu.get_barrier_semaphore()

    def greet_tile(s, c):
        pl.semaphore_signal(barrier, inc=1, device_id={"tile": lax.rem(me + s, n_tile)}, device_id_type=MESH)
        return c

    def greet_rep(s, c):
        pl.semaphore_signal(barrier, inc=1, device_id={"rep": lax.rem(rep + s, n_rep)}, device_id_type=MESH)
        return c

    def greet_mate(s, c):
        where = {"tile": mate, "rep": lax.rem(rep + s, n_rep)}
        pl.semaphore_signal(barrier, inc=1, device_id=where, device_id_type=MESH)
        return c

    lax.fori_loop(1, n_tile, greet_tile, 0)
    lax.fori_loop(1, n_rep, greet_rep, 0)
    lax.fori_loop(1, n_rep, greet_mate, 0)

    gi = lax.broadcasted_iota(jnp.int32, (C_OUT, C_OUT), 0) >> 3
    gj = lax.broadcasted_iota(jnp.int32, (C_OUT, C_OUT), 1) >> 3
    same_group = (gi == gj).astype(F32)

    def exact(v, w):
        return jnp.dot(v, w, precision=lax.Precision.HIGHEST, preferred_element_type=F32)

    def per_group(v):
        return exact(v, same_group)

    def packed(rows):
        ch = lax.broadcasted_iota(jnp.int32, (C_OUT, 128), 0) >> 3
        lane = lax.broadcasted_iota(jnp.int32, (C_OUT, 128), 1)
        return sum(exact(rows[k], (lane == ch + k * GROUPS).astype(F32)) for k in range(CLIPS))

    def unpacked(v, k):
        lane = lax.broadcasted_iota(jnp.int32, (128, C_OUT), 0)
        ch = lax.broadcasted_iota(jnp.int32, (128, C_OUT), 1) >> 3
        return exact(v, (lane == ch + k * GROUPS).astype(F32))

    def greeted():
        pl.semaphore_wait(barrier, n_tile + 2 * n_rep - 3)

    land, tile_rows, drain = exchange(n_tile, me, greeted, strip, mine, meta, *moving)

    def forward(n, c):
        acc = None
        for p in range(0, 27, 2):
            rows = jnp.concatenate([pair_slab(even, odd, n * 4 + j, p) for j in range(4)], axis=0)
            d = jnp.dot(rows, filt[p * C_IN : min(p + 2, 27) * C_IN, :], preferred_element_type=F32)
            acc = d if acc is None else acc + d
        for j in range(4):
            one = acc[j * VOX : (j + 1) * VOX]
            conv[n * 4 + j] = one
            sums[pl.ds(n * 4 + j, 1), :] = jnp.sum(one, axis=0, keepdims=True)
        return c

    for h in range(2):
        land(h)

        def unpack(j, c):
            shifted(h * PART + j, tile_rows(h, j), even, odd)
            return c

        lax.fori_loop(0, PART, unpack, 0)
        lax.fori_loop(h * PART // 4, (h + 1) * PART // 4, forward, 0)
    drain()

    gsum = per_group(sums[...])
    tmean[...] = gsum / GVOX

    def centre(i, c):
        d = conv[i] - tmean[pl.ds(i, 1), :]
        sq[pl.ds(i, 1), :] = jnp.sum(d * d, axis=0, keepdims=True)
        return c

    lax.fori_loop(0, WSLOTS, centre, 0)
    local = []
    for k in range(CLIPS):
        m = member[k]
        n_k = jnp.sum(m, axis=0, keepdims=True)
        mu = jnp.sum(m * gsum, axis=0, keepdims=True) / (GVOX * jnp.maximum(n_k, 1.0))
        off = tmean[...] - mu
        first = jnp.sum(m * sums[...], axis=0, keepdims=True)
        second = jnp.sum(m * (sq[...] + float(VOX) * off * off), axis=0, keepdims=True)
        local.append(jnp.concatenate([n_k / float(CPG), first, second, jnp.zeros((5, C_OUT), F32)], axis=0))
    blk[...] = packed(local)

    gather_block(blk, buf, g_send, g_recv, me, n_tile)

    all_n = buf[:, 0:1, :]
    all_s = buf[:, 1:2, :]
    n_tot = jnp.maximum(jnp.sum(all_n, axis=0), 1.0)
    mean = jnp.sum(all_s, axis=0) / (GVOX * n_tot)
    off = all_s / (GVOX * jnp.maximum(all_n, 1.0)) - mean
    var = jnp.sum(buf[:, 2:3, :] + GVOX * all_n * off * off, axis=0) / (GVOX * n_tot)
    table = jnp.concatenate([mean, lax.rsqrt(var + epsilon), jnp.zeros((6, 128), F32)], axis=0)
    wide_table = [unpacked(table, k) for k in range(CLIPS)]
    tmean[...] = sum(member[k] * wide_table[k][0:1] for k in range(CLIPS))
    tinv[...] = sum(member[k] * wide_table[k][1:2] for k in range(CLIPS))

    gain = affine[0:1, :]
    shift = affine[1:2, :]

    def middle(i, c):
        mu = tmean[pl.ds(i, 1), :]
        iv = tinv[pl.ds(i, 1), :]
        first = jnp.zeros((1, C_OUT), F32)
        cross = jnp.zeros((1, C_OUT), F32)
        for r in range(0, VOX, 64):
            normed = (conv[i, r : r + 64, :] - mu) * iv
            pre = normed * gain + shift
            sg = 1.0 / (1.0 + jnp.exp(-pre))
            act[i, r : r + 64, :] = (pre * sg).astype(BF16)
            pg = (up[i, r : r + 64, :].astype(F32) * loss_scale) * sg * (1.0 + pre * (1.0 - sg))
            first += jnp.sum(pg, axis=0, keepdims=True)
            cross += jnp.sum(pg * normed, axis=0, keepdims=True)
            conv[i, r : r + 64, :] = normed
            ngrad[i, r : r + 64, :] = pg * gain
        sums[pl.ds(i, 1), :] = first
        sq[pl.ds(i, 1), :] = cross
        return c

    lax.fori_loop(0, WSLOTS, middle, 0)
    firsts = [jnp.sum(member[k] * sums[...], axis=0, keepdims=True) for k in range(CLIPS)]
    crosses = [jnp.sum(member[k] * sq[...], axis=0, keepdims=True) for k in range(CLIPS)]
    zeros = jnp.zeros((6, C_OUT), F32)
    scaled = packed([jnp.concatenate([firsts[k] * gain, crosses[k] * gain, zeros], axis=0) for k in range(CLIPS)])
    over_clips = [sum(crosses), sum(firsts)]
    halves = [v[:, lo : lo + 128] for v in over_clips for lo in (0, 128)]
    blk2[...] = jnp.concatenate([scaled[0:2]] + halves + [jnp.zeros((2, 128), F32)], axis=0)
    gather_block(blk2, buf2, h_send, h_recv, me, n_tile)
    total = jnp.sum(buf2[...], axis=0)

    nbuf[rep] = total

    def norm_start(s, c):
        to = lax.rem(rep + s, n_rep)
        remote(nbuf.at[rep], nbuf.at[rep], n_send.at[s], n_recv.at[rep], rep=to).start()
        return c

    def norm_wait(s, c):
        to = lax.rem(rep + s, n_rep)
        remote(nbuf.at[rep], nbuf.at[rep], n_send.at[s], n_recv.at[to], rep=to).wait_send()
        remote(nbuf.at[rep], nbuf.at[to], n_send.at[s], n_recv.at[to], rep=to).wait_recv()
        return c

    lax.fori_loop(1, n_rep, norm_start, 0)

    table = total / (GVOX * n_tot)
    wide_table = [unpacked(table, k) for k in range(CLIPS)]
    sums[...] = sum(member[k] * wide_table[k][0:1] for k in range(CLIPS))
    sq[...] = sum(member[k] * wide_table[k][1:2] for k in range(CLIPS))

    def conv_gradient(i, c):
        iv = tinv[pl.ds(i, 1), :]
        m1 = sums[pl.ds(i, 1), :]
        m2 = sq[pl.ds(i, 1), :]
        for r in range(0, VOX, 64):
            g = iv * (ngrad[i, r : r + 64, :] - m1 - conv[i, r : r + 64, :] * m2)
            cgrad[i, r : r + 64, :] = g.astype(BF16)
        return c

    lax.fori_loop(0, WSLOTS, conv_gradient, 0)

    share = ROWS // chips

    batches = [(0, 8), (8, 16), (16, 22), (22, 27)]

    def mate_copy(b):
        lo, hi = batches[b]
        rows = pl.ds(lo * C_IN, (hi - lo) * C_IN)
        return remote(half.at[1 - core, rows], other.at[rows], c_send.at[b], c_recv.at[b], tile=mate)

    row, col = lax.div(chip, SIDE), lax.rem(chip, SIDE)
    u = col + core * (row - col)
    v = row + core * (col - row)

    def chip_at(pu, pv):
        return pu * (1 + (SIDE - 1) * core) + pv * (SIDE - (SIDE - 1) * core)

    def place(j):
        return j % SIDE + core * (j // SIDE - j % SIDE), j // SIDE + core * (j % SIDE - j // SIDE)

    def ring_copy(j, slot, pu, pv):
        to = chip_at(pu, v) * 2 + core
        at = slot * SIDE + pv
        return remote(half.at[core, pl.ds(j * share, share)], part.at[at], p_send.at[j], p_recv.at[at], tile=to)

    def cross_copy(slot, pv):
        to = chip_at(u, pv) * 2 + core
        return remote(ring.at[pv], part2.at[slot], r_send.at[pv], r_recv.at[slot], tile=to)

    done = [0]

    def settle(b):
        lo, hi = batches[b][0] * C_IN, batches[b][1] * C_IN
        mate_copy(b).wait_recv()
        half[core, lo:hi, :] = half[core, lo:hi, :] + other[lo:hi, :]
        while (done[0] + 1) * share <= hi:
            j = done[0]

            pu, pv = place(j)

            @pl.when(pu != u)
            def _():
                ring_copy(j, u, pu, pv).start()

            @pl.when(pu == u)
            def _():
                part[u * SIDE + pv] = half[core, j * share : (j + 1) * share, :]

            done[0] += 1

    for b, (first_tap, end_tap) in enumerate(batches):
        for p in range(first_tap, end_tap, 2):
            d = None
            for n in range(0, WSLOTS, 4):
                rows = jnp.concatenate([pair_slab(even, odd, i, p) for i in range(n, n + 4)], axis=0)
                g = jnp.concatenate([cgrad[i] for i in range(n, n + 4)], axis=0)
                t = lax.dot_general(rows, g, (((0,), (0,)), ((), ())), preferred_element_type=F32)
                d = t if d is None else d + t
            lo, hi = p * C_IN, min(p + 2, 27) * C_IN
            half[0, lo:hi, :] = d[:, :128]
            half[1, lo:hi, :] = d[:, 128:]
        mate_copy(b).start()
        if b > 0:
            settle(b - 1)
    settle(len(batches) - 1)

    def ring_sum(s, c):
        pv = lax.rem(v + s, SIDE)
        for t in range(1, SIDE):
            pu = lax.rem(u + t, SIDE)
            ring_copy(0, pu, pu, pv).wait_recv()
        ring[pv] = sum(part[pu * SIDE + pv] for pu in range(SIDE))

        @pl.when(pv != v)
        def _():
            cross_copy(v, pv).start()

        @pl.when(pv == v)
        def _():
            part2[v] = ring[v]

        return c

    lax.fori_loop(1, SIDE + 1, ring_sum, 0)
    for j in range(chips):
        pu, pv = place(j)

        @pl.when(pu != u)
        def _():
            ring_copy(j, u, pu, pv).wait_send()

    for b in range(len(batches)):
        mate_copy(b).wait_send()

    def cross_wait(s, c):
        pv = lax.rem(v + s, SIDE)
        cross_copy(v, pv).wait_send()
        cross_copy(pv, pv).wait_recv()
        return c

    lax.fori_loop(1, SIDE, cross_wait, 0)

    piece = red.shape[0] // n_rep
    red[0:share, :] = jnp.sum(part2[...], axis=0)
    if red.shape[0] > share:
        red[share:, :] = jnp.zeros((red.shape[0] - share, 128), F32)
    zin[rep] = red[pl.ds(pl.multiple_of(rep * piece, 8), piece), :]

    def z_copy(to, slot, s):
        return remote(red.at[pl.ds(pl.multiple_of(to * piece, 8), piece)], zin.at[slot], z_send.at[s], z_recv.at[slot], rep=to)

    def rows_at(r):
        return pl.ds(pl.multiple_of(r * piece, 8), piece)

    def y_copy(side, to, slot, s):
        tile = me if side == 0 else mate
        from_core = core if side == 0 else 1 - core
        mine = zout.at[core, rows_at(rep)]
        there = zout.at[core, rows_at(rep)] if slot is None else zout.at[from_core, rows_at(slot)]
        got = core * n_rep + rep if slot is None else from_core * n_rep + slot
        return remote(mine, there, y_send.at[side * n_rep + s], y_recv.at[got], tile=tile, rep=to)

    def each(what):
        def body(s, c):
            what(lax.rem(rep + s, n_rep), s)
            return c

        lax.fori_loop(1, n_rep, body, 0)

    each(lambda to, s: z_copy(to, rep, s).start())
    lax.fori_loop(1, n_rep, norm_wait, 0)
    norm[...] = jnp.sum(nbuf[...], axis=0)
    each(lambda to, s: z_copy(to, rep, s).wait_send())
    each(lambda to, s: z_copy(to, to, s).wait_recv())
    zout[core, rows_at(rep), :] = jnp.sum(zin[...], axis=0)
    y_copy(1, rep, None, 0).start()
    for side in range(2):
        each(lambda to, s: y_copy(side, to, None, s).start())
    y_copy(1, rep, None, 0).wait_send()
    y_copy(1, rep, rep, 0).wait_recv()
    for side in range(2):
        each(lambda to, s: y_copy(side, to, None, s).wait_send())
        each(lambda to, s: y_copy(side, to, to, s).wait_recv())

    keep = grad.shape[0]
    own = pl.ds(pl.multiple_of(core * (share - keep), 8), keep)
    grad[:, 0:128] = zout[0, own, :]
    grad[:, 128:256] = zout[1, own, :]


def main_call(n_tile, n_rep, strip, mine, meta, filt, up, member, affine):
    lines = n_tile * TH
    depth = lines // RMOD + 2
    chips = n_tile // 2
    share = ROWS // chips
    keep = share // 2 + 4 if (share // 2) % 8 else share // 2
    padded = -(-share // (8 * n_rep)) * 8 * n_rep
    whole = pl.BlockSpec(memory_space=pltpu.VMEM)
    dma = pltpu.SemaphoreType.DMA
    return pl.pallas_call(
        partial(main_kernel, n_tile, n_rep),
        out_shape=(
            jax.ShapeDtypeStruct((WSLOTS, VOX, C_OUT), BF16),
            jax.ShapeDtypeStruct((keep, C_OUT), F32),
            jax.ShapeDtypeStruct((8, 128), F32),
        ),
        in_specs=[pl.BlockSpec(memory_space=pl.ANY), whole, pl.BlockSpec(memory_space=pltpu.SMEM)] + [whole] * 4,
        out_specs=(whole,) * 3,
        scratch_shapes=[
            pltpu.VMEM((3, WSLOTS, 480, C_IN), BF16),
            pltpu.VMEM((3, WSLOTS, 384, C_IN), BF16),
            pltpu.VMEM((WSLOTS, VOX, C_OUT), F32),
            pltpu.VMEM((WSLOTS, VOX, C_OUT), F32),
            pltpu.VMEM((WSLOTS, VOX, C_OUT), BF16),
            pltpu.VMEM((WSLOTS, C_OUT), F32),
            pltpu.VMEM((WSLOTS, C_OUT), F32),
            pltpu.VMEM((WSLOTS, C_OUT), F32),
            pltpu.VMEM((WSLOTS, C_OUT), F32),
            pltpu.VMEM((8, 128), F32),
            pltpu.VMEM((n_tile, 8, 128), F32),
            pltpu.VMEM((2, ROWS, 128), F32),
            pltpu.VMEM((ROWS, 128), F32),
            pltpu.VMEM((chips, share, 128), F32),
            pltpu.VMEM((SIDE, share, 128), F32),
            pltpu.VMEM((SIDE, share, 128), F32),
            pltpu.VMEM((padded, 128), F32),
            pltpu.VMEM((n_rep, padded // n_rep, 128), F32),
            pltpu.VMEM((2, padded, 128), F32),
            pltpu.VMEM((n_rep, 8, 128), F32),
            pltpu.VMEM((8, 128), F32),
            pltpu.VMEM((n_tile, 8, 128), F32),
        ]
        + [dma((n_tile,))] * 4
        + [dma((14,))] * 2
        + [dma((chips,))] * 2
        + [dma((SIDE,))] * 2
        + [dma((n_rep,))] * 2
        + [dma((2 * n_rep,))] * 2
        + [dma((n_rep,))] * 2
        + [
            pltpu.VMEM((n_tile, 1, 128), jnp.int32),
            pltpu.SMEM((n_tile, 1, 128), jnp.int32),
            pltpu.VMEM((PLANES, lines // RMOD + 1, 8 * WBLK, C_IN), BF16),
            pltpu.VMEM(((PLANES + 1) * depth, WBLK + 1, 8, C_IN), F32),
            pltpu.VMEM((PART * PIECE, C_IN), F32),
            pltpu.VMEM((n_tile * 2, PART * PIECE, C_IN), BF16),
            pltpu.VMEM((STOPS * 2, PART * PIECE, C_IN), BF16),
            pltpu.VMEM((STOPS * 2 * PART, 16, C_IN), F32),
            dma((n_tile,)),
            dma((n_tile,)),
            dma,
            dma((TH * FMOD,)),
            dma((lines // RMOD + 1,)),
            dma((TH,)),
            dma((n_tile * 2,)),
            dma((STOPS * 2,)),
        ],
        compiler_params=pltpu.CompilerParams(collective_id=0, has_side_effects=True, vmem_limit_bytes=VMEM_BYTES),
        cost_estimate=pl.CostEstimate(flops=4 * WSLOTS * VOX * ROWS * C_OUT, bytes_accessed=16 * 1024 * 1024, transcendentals=WSLOTS * VOX * C_OUT),
        name="conv_norm",
    )(strip, mine, meta, filt, up, member, affine)


def shards(
    input_video,
    block_clip,
    send_slot,
    recv_index,
    tile_clip,
    kernel,
    norm_gain,
    norm_shift,
    upstream,
):
    peer_count = lax.axis_size("tile")
    me = lax.axis_index("tile")
    strip = input_video[0].reshape(PLANES, FMOD, TH, 8 * WBLK, C_IN)
    clip_ids = block_clip[0]
    mine = jnp.concatenate(
        [send_slot[0, 0].reshape(-1), recv_index[0, 0], jnp.zeros((128 - 2 * peer_count - WSLOTS,), jnp.int32)]
    )[None]
    depth = peer_count * TH // RMOD + 2
    block = jnp.arange(TBLK, dtype=jnp.int32)
    place = (me % FMOD - TT * block + 2) % FMOD
    linked = jnp.concatenate([jnp.zeros((1,), bool), clip_ids[1:] == clip_ids[:-1]])
    plane = jnp.where((place >= 2) | linked, (TT * block - 2 + place) // FMOD, PLANES)
    owner = jnp.arange(peer_count, dtype=jnp.int32)
    top = owner * TH - 1
    line = (top + (me // FMOD - top) % RMOD - me // FMOD + RMOD) // RMOD
    meta = jnp.concatenate(
        [plane * depth, jnp.zeros((2,), jnp.int32), line, jnp.zeros((120 - peer_count,), jnp.int32)]
    )[None]
    clips = jnp.arange(CLIPS, dtype=jnp.int32)[:, None, None]
    member = jnp.broadcast_to((tile_clip[0, 0][None, :, None] == clips).astype(F32), (CLIPS, WSLOTS, C_OUT))
    affine = jnp.concatenate([norm_gain[None], norm_shift[None], jnp.zeros((6, C_OUT), F32)], axis=0)
    activation, grad_rows, norm_rows = main_call(
        peer_count, lax.axis_size("rep"), strip, mine, meta, kernel, upstream[0, 0], member, affine
    )
    row_share = ROWS // peer_count
    skip = (grad_rows.shape[0] - row_share) * lax.rem(lax.axis_index("tile"), 2)
    grad_shard = lax.dynamic_slice_in_dim(grad_rows, skip, row_share, 0)
    return (activation[None, None], grad_shard, norm_rows[2:6].reshape(2, C_OUT))


def solution(mesh):
    placed = (
        P("rep", None, "tile", None, None),
        P("rep", None),
        P("rep", "tile", None, None),
        P("rep", "tile", None),
        P("rep", "tile", None),
        P(),
        P(),
        P(),
        P("rep", "tile", None, None, None),
    )
    return jax.shard_map(
        shards,
        mesh=mesh,
        in_specs=placed,
        out_specs=(P("rep", "tile", None, None, None), P("tile", None), P()),
        check_vma=False,
    )
```

```python
from functools import partial

import jax
import jax.numpy as jnp
from jax import lax
from jax.experimental import pallas as pl
from jax.experimental.pallas import tpu as pltpu
from jax.sharding import PartitionSpec as P

C_IN = 128
C_OUT = 256
GROUPS = 32
CPG = 8
TT = 4
TH = 8
TW = 8
TBLK = 6
CLIPS = 3
WBLK = 8
WSLOTS = 16
VOX = 256
FRAMES = 24


epsilon = 1e-05


MESH = pl.DeviceIdType.MESH
TAP = [(a, e, q) for a in range(3) for e in range(3) for q in range(3)]
F32, BF16 = jnp.float32, jnp.bfloat16
ROWS = 27 * C_IN
SIDE = 4
GVOX = float(VOX * CPG)
SLAB = 60 * 8
VMEM_BYTES = 60 * 1024 * 1024


def remote(src, dst, send, recv, **where):
    return pltpu.make_async_remote_copy(
        src_ref=src, dst_ref=dst, send_sem=send, recv_sem=recv, device_id=where, device_id_type=MESH
    )


def gather_block(block, buf, send, recv, me, count):
    buf[me] = block[...]

    def start(s, c):
        to = lax.rem(me + s, count)
        remote(block, buf.at[me], send.at[s], recv.at[me], tile=to).start()
        return c

    def wait(s, c):
        to = lax.rem(me + s, count)
        remote(block, buf.at[me], send.at[s], recv.at[to], tile=to).wait_send()
        remote(block, buf.at[to], send.at[s], recv.at[to], tile=to).wait_recv()
        return c

    lax.fori_loop(1, count, start, 0)
    lax.fori_loop(1, count, wait, 0)


def shifted(i, x, even, odd):
    for q in range(3):
        y = x[:, :, q : q + 8, :]
        even[q, i] = y.reshape(480, C_IN).astype(BF16)
        odd[q, i] = y[:, 1:9].reshape(384, C_IN).astype(BF16)


def tap_slab(even, odd, i, tap):
    a, e, q = tap
    out = []
    for f in range(TT):
        if e == 1:
            out.append(odd[q, i, pl.ds((f + a) * 64, 64), :])
        else:
            out.append(even[q, i, pl.ds((f + a) * 80 + e * 8, 64), :])
    return jnp.concatenate(out, axis=0)


def pair_slab(even, odd, i, p):
    left = tap_slab(even, odd, i, TAP[p])
    if p + 1 == len(TAP):
        return left
    return jnp.concatenate([left, tap_slab(even, odd, i, TAP[p + 1])], axis=1)


FMOD = 6
RMOD = 5
STOPS = FMOD * RMOD
PIECE = 20
PARTS = 2
PART = WSLOTS // PARTS
PLANES = FRAMES // FMOD


def ordered_peer(me, s):
    core, chip = lax.rem(me, 2), lax.div(me, 2)
    row, col = lax.div(chip, SIDE), lax.rem(chip, SIDE)
    n = lax.div(s, 2)
    p, q = lax.rem(n, SIDE), lax.rem(n + lax.div(n, SIDE), SIDE)
    x = lax.rem(col + p + core * (q - p), SIDE)
    y = lax.rem(row + q + core * (p - q), SIDE)
    return (y * SIDE + x) * 2 + lax.rem(core + lax.rem(s, 2), 2)


def exchange(
    n_tile, me, greeted, strip, mine, meta,
    tab, stab, raw, wide, stage, sendb, recvb, rows32,
    t_send, t_recv, s_sem, v_send, v_recv, v_own, w_send, w_recv,
):
    lines = n_tile * TH
    my_f = lax.rem(me, FMOD)
    my_r = lax.div(me, FMOD)
    depth = lines // RMOD + 2
    tab[me] = mine[...]
    greeted()

    def table(to, slot, s):
        return remote(mine, tab.at[slot], t_send.at[s], t_recv.at[slot], tile=to)

    def table_start(s, c):
        table(lax.rem(me + s, n_tile), me, s).start()
        return c

    def table_wait(s, c):
        to = lax.rem(me + s, n_tile)
        table(to, me, s).wait_send()
        table(to, to, s).wait_recv()
        return c

    lax.fori_loop(1, n_tile, table_start, 0)

    def lines_to(to, what):
        a = lax.rem(to, FMOD)
        h0 = lax.rem(lax.div(to, FMOD) + RMOD * TH - lax.rem(me * TH, RMOD), RMOD)

        @pl.when(to < STOPS)
        def _():
            what(a, h0, lax.div(me * TH + h0, RMOD))

            @pl.when(h0 < TH - RMOD)
            def _():
                what(a, h0 + RMOD, lax.div(me * TH + h0 + RMOD, RMOD))

    def line_copy(to, a, h, index):
        return remote(strip.at[:, a, h], raw.at[:, index], v_send.at[h * FMOD + a], v_recv.at[index], tile=to)

    def spread(s, c):
        to = ordered_peer(me, s)
        lines_to(to, lambda a, h, index: line_copy(to, a, h, index).start())
        return c

    def keep(a, h, index):
        pltpu.make_async_copy(strip.at[:, a, h], raw.at[:, index], v_own.at[h]).start()

    lax.fori_loop(1, n_tile, spread, 0)
    lines_to(me, keep)

    def clear(i, c):
        wide[i] = jnp.zeros(wide.shape[1:], F32)
        return c

    lax.fori_loop(0, wide.shape[0], clear, 0)

    lax.fori_loop(1, n_tile, table_wait, 0)
    scalars = pltpu.make_async_copy(tab, stab, s_sem)
    scalars.start()

    @pl.when(me < STOPS)
    def _():
        def arrive(i, c):
            y = i * RMOD + my_r
            owner = lax.div(y, TH)
            h = lax.rem(y, TH)

            @pl.when(owner != me)
            def _():
                remote(strip.at[:, my_f, h], raw.at[:, i], v_send.at[0], v_recv.at[i], tile=owner).wait_recv()

            @pl.when(owner == me)
            def _():
                pltpu.make_async_copy(strip.at[:, my_f, h], raw.at[:, i], v_own.at[h]).wait()

            for k in range(PLANES):
                line = raw[k, i].astype(F32)
                gap = jnp.zeros((1, C_IN), F32)
                line = jnp.concatenate([gap, line, gap, jnp.zeros((6, C_IN), F32)], axis=0)
                wide[k * depth + i + 1] = line.reshape(WBLK + 1, 8, C_IN)
            return c

        lax.fori_loop(0, lax.div(lines - my_r + RMOD - 1, RMOD), arrive, 0)

    scalars.wait()

    def part_copy(w, slot, h):
        return remote(sendb.at[w * PARTS + h], recvb.at[slot * PARTS + h], w_send.at[w * PARTS + h], w_recv.at[slot * PARTS + h], tile=w)

    @pl.when(me < STOPS)
    def _():
        def serve(step, c):
            h = lax.div(step, n_tile)
            w = ordered_peer(me, lax.rem(step + 1, n_tile))
            for j in range(PART):
                r = stab[w, 0, 64 + h * PART + j]
                t = lax.div(r, 2)
                slot = stab[t, 0, w * 2 + lax.rem(r, 2)]
                base = meta[0, lax.div(slot, WBLK)] + meta[0, 8 + t]
                first = lax.rem(slot, WBLK)
                for half in range(2):
                    at = j * PIECE + half * 10
                    stage[at : at + 8, :] = wide[base + half, first]
                    stage[at + 8 : at + 10, :] = wide[base + half, first + 1][:2]
            sendb[w * PARTS + h] = stage[...].astype(BF16)

            @pl.when(w != me)
            def _():
                part_copy(w, me, h).start()

            @pl.when(w == me)
            def _():
                recvb[me * PARTS + h] = sendb[me * PARTS + h]

            return c

        lax.fori_loop(0, PARTS * n_tile, serve, 0)

    def land(h):
        def body(s, c):
            i = ordered_peer(me, lax.rem(s, n_tile))

            @pl.when(i < STOPS)
            def _():
                @pl.when(i != me)
                def _():
                    part_copy(i, i, h).wait_recv()

                v = recvb[i * PARTS + h].astype(F32)
                for j in range(PART):
                    for half in range(2):
                        at = j * PIECE + half * 10
                        rows32[i * 2 * PART + j * 2 + half, 0:10, :] = v[at : at + 10]

            return c

        lax.fori_loop(1, n_tile + 1, body, 0)

    def tile_rows(h, j):
        r = stab[me, 0, 64 + h * PART + j]
        t = lax.div(r, 2)
        b = lax.div(stab[t, 0, me * 2 + lax.rem(r, 2)], WBLK)
        out = []
        for f in range(TT + 2):
            a = lax.rem(b * TT + TT + f, FMOD)
            for y in range(TH + 2):
                q = lax.rem(t * TH + 4 + y % RMOD, RMOD)
                at = (q * FMOD + a) * (2 * PART) + j * 2 + y // RMOD
                out.append(rows32[at, 0:10, :])
        return jnp.stack(out, axis=0).reshape(TT + 2, TH + 2, TW + 2, C_IN)

    def drain():
        def sent(s, c):
            to = ordered_peer(me, s)
            lines_to(to, lambda a, h, index: line_copy(to, a, h, index).wait_send())
            return c

        lax.fori_loop(1, n_tile, sent, 0)

        @pl.when(me < STOPS)
        def _():
            def served(s, c):
                w = lax.rem(me + s, n_tile)
                for h in range(PARTS):
                    part_copy(w, me, h).wait_send()
                return c

            lax.fori_loop(1, n_tile, served, 0)

    return land, tile_rows, drain


def main_kernel(
    n_tile, n_rep, strip, mine, meta, filt_hbm, up_hbm, clips, gains, shifts, act, grad, norm,
    filt, up, member, load_sem, even, odd, conv, ngrad, cgrad, sums, sq, tmean, tinv, blk, buf, half, other, part, ring, part2, red, zin, zout, nbuf, blk2, buf2,
    g_send, g_recv, h_send, h_recv, c_send, c_recv, p_send, p_recv, r_send, r_recv, z_send, z_recv, y_send, y_recv, n_send, n_recv, *moving,
):
    me = lax.axis_index("tile")
    rep = lax.axis_index("rep")
    core = lax.rem(me, 2)
    chip = lax.div(me, 2)
    chips = n_tile // 2
    mate = chip * 2 + 1 - core
    loss_scale = float(n_rep * n_tile * WSLOTS * VOX) ** (-0.5)

    barrier = pltpu.get_barrier_semaphore()

    def greet_tile(s, c):
        pl.semaphore_signal(barrier, inc=1, device_id={"tile": lax.rem(me + s, n_tile)}, device_id_type=MESH)
        return c

    def greet_rep(s, c):
        pl.semaphore_signal(barrier, inc=1, device_id={"rep": lax.rem(rep + s, n_rep)}, device_id_type=MESH)
        return c

    def greet_mate(s, c):
        where = {"tile": mate, "rep": lax.rem(rep + s, n_rep)}
        pl.semaphore_signal(barrier, inc=1, device_id=where, device_id_type=MESH)
        return c

    lax.fori_loop(1, n_tile, greet_tile, 0)
    lax.fori_loop(1, n_rep, greet_rep, 0)
    lax.fori_loop(1, n_rep, greet_mate, 0)

    gi = lax.broadcasted_iota(jnp.int32, (C_OUT, C_OUT), 0) >> 3
    gj = lax.broadcasted_iota(jnp.int32, (C_OUT, C_OUT), 1) >> 3
    same_group = (gi == gj).astype(F32)

    def exact(v, w):
        return jnp.dot(v, w, precision=lax.Precision.HIGHEST, preferred_element_type=F32)

    def per_group(v):
        return exact(v, same_group)

    def packed(rows):
        ch = lax.broadcasted_iota(jnp.int32, (C_OUT, 128), 0) >> 3
        lane = lax.broadcasted_iota(jnp.int32, (C_OUT, 128), 1)
        return sum(exact(rows[k], (lane == ch + k * GROUPS).astype(F32)) for k in range(CLIPS))

    def unpacked(v, k):
        lane = lax.broadcasted_iota(jnp.int32, (128, C_OUT), 0)
        ch = lax.broadcasted_iota(jnp.int32, (128, C_OUT), 1) >> 3
        return exact(v, (lane == ch + k * GROUPS).astype(F32))

    def greeted():
        pl.semaphore_wait(barrier, n_tile + 2 * n_rep - 3)

    load_filt = pltpu.make_async_copy(filt_hbm, filt, load_sem.at[0])
    load_up = pltpu.make_async_copy(up_hbm, up, load_sem.at[1])
    load_filt.start()
    load_up.start()
    for k in range(CLIPS):
        member[k] = jnp.broadcast_to((clips[...] == k).astype(F32), (WSLOTS, C_OUT))

    land, tile_rows, drain = exchange(n_tile, me, greeted, strip, mine, meta, *moving)

    def forward(n, c):
        acc = None
        for p in range(0, 27, 2):
            rows = jnp.concatenate([pair_slab(even, odd, n * 4 + j, p) for j in range(4)], axis=0)
            d = jnp.dot(rows, filt[p * C_IN : min(p + 2, 27) * C_IN, :], preferred_element_type=F32)
            acc = d if acc is None else acc + d
        for j in range(4):
            one = acc[j * VOX : (j + 1) * VOX]
            conv[n * 4 + j] = one
            sums[pl.ds(n * 4 + j, 1), :] = jnp.sum(one, axis=0, keepdims=True)
        return c

    load_filt.wait()
    load_up.wait()
    for h in range(PARTS):
        land(h)

        def unpack(j, c):
            shifted(h * PART + j, tile_rows(h, j), even, odd)
            return c

        lax.fori_loop(0, PART, unpack, 0)
        lax.fori_loop(h * PART // 4, (h + 1) * PART // 4, forward, 0)
    drain()

    gsum = per_group(sums[...])
    tmean[...] = gsum / GVOX

    def centre(i, c):
        d = conv[i] - tmean[pl.ds(i, 1), :]
        sq[pl.ds(i, 1), :] = jnp.sum(d * d, axis=0, keepdims=True)
        return c

    lax.fori_loop(0, WSLOTS, centre, 0)
    local = []
    for k in range(CLIPS):
        m = member[k]
        n_k = jnp.sum(m, axis=0, keepdims=True)
        mu = jnp.sum(m * gsum, axis=0, keepdims=True) / (GVOX * jnp.maximum(n_k, 1.0))
        off = tmean[...] - mu
        first = jnp.sum(m * sums[...], axis=0, keepdims=True)
        second = jnp.sum(m * (sq[...] + float(VOX) * off * off), axis=0, keepdims=True)
        local.append(jnp.concatenate([n_k / float(CPG), first, second, jnp.zeros((5, C_OUT), F32)], axis=0))
    blk[...] = packed(local)

    gather_block(blk, buf, g_send, g_recv, me, n_tile)

    all_n = buf[:, 0:1, :]
    all_s = buf[:, 1:2, :]
    n_tot = jnp.maximum(jnp.sum(all_n, axis=0), 1.0)
    mean = jnp.sum(all_s, axis=0) / (GVOX * n_tot)
    off = all_s / (GVOX * jnp.maximum(all_n, 1.0)) - mean
    var = jnp.sum(buf[:, 2:3, :] + GVOX * all_n * off * off, axis=0) / (GVOX * n_tot)
    table = jnp.concatenate([mean, lax.rsqrt(var + epsilon), jnp.zeros((6, 128), F32)], axis=0)
    wide_table = [unpacked(table, k) for k in range(CLIPS)]
    tmean[...] = sum(member[k] * wide_table[k][0:1] for k in range(CLIPS))
    tinv[...] = sum(member[k] * wide_table[k][1:2] for k in range(CLIPS))

    gain = gains[...]
    shift = shifts[...]

    def middle(i, c):
        mu = tmean[pl.ds(i, 1), :]
        iv = tinv[pl.ds(i, 1), :]
        first = jnp.zeros((1, C_OUT), F32)
        cross = jnp.zeros((1, C_OUT), F32)
        for r in range(0, VOX, 64):
            normed = (conv[i, r : r + 64, :] - mu) * iv
            pre = normed * gain + shift
            sg = 1.0 / (1.0 + jnp.exp(-pre))
            act[i, r : r + 64, :] = (pre * sg).astype(BF16)
            pg = (up[i, r : r + 64, :].astype(F32) * loss_scale) * sg * (1.0 + pre * (1.0 - sg))
            first += jnp.sum(pg, axis=0, keepdims=True)
            cross += jnp.sum(pg * normed, axis=0, keepdims=True)
            conv[i, r : r + 64, :] = normed
            ngrad[i, r : r + 64, :] = pg * gain
        sums[pl.ds(i, 1), :] = first
        sq[pl.ds(i, 1), :] = cross
        return c

    lax.fori_loop(0, WSLOTS, middle, 0)
    firsts = [jnp.sum(member[k] * sums[...], axis=0, keepdims=True) for k in range(CLIPS)]
    crosses = [jnp.sum(member[k] * sq[...], axis=0, keepdims=True) for k in range(CLIPS)]
    zeros = jnp.zeros((6, C_OUT), F32)
    scaled = packed([jnp.concatenate([firsts[k] * gain, crosses[k] * gain, zeros], axis=0) for k in range(CLIPS)])
    over_clips = [sum(crosses), sum(firsts)]
    halves = [v[:, lo : lo + 128] for v in over_clips for lo in (0, 128)]
    blk2[...] = jnp.concatenate([scaled[0:2]] + halves + [jnp.zeros((2, 128), F32)], axis=0)
    gather_block(blk2, buf2, h_send, h_recv, me, n_tile)
    total = jnp.sum(buf2[...], axis=0)

    nbuf[rep] = total

    def norm_start(s, c):
        to = lax.rem(rep + s, n_rep)
        remote(nbuf.at[rep], nbuf.at[rep], n_send.at[s], n_recv.at[rep], rep=to).start()
        return c

    def norm_wait(s, c):
        to = lax.rem(rep + s, n_rep)
        remote(nbuf.at[rep], nbuf.at[rep], n_send.at[s], n_recv.at[to], rep=to).wait_send()
        remote(nbuf.at[rep], nbuf.at[to], n_send.at[s], n_recv.at[to], rep=to).wait_recv()
        return c

    lax.fori_loop(1, n_rep, norm_start, 0)

    table = total / (GVOX * n_tot)
    wide_table = [unpacked(table, k) for k in range(CLIPS)]
    sums[...] = sum(member[k] * wide_table[k][0:1] for k in range(CLIPS))
    sq[...] = sum(member[k] * wide_table[k][1:2] for k in range(CLIPS))

    def conv_gradient(i, c):
        iv = tinv[pl.ds(i, 1), :]
        m1 = sums[pl.ds(i, 1), :]
        m2 = sq[pl.ds(i, 1), :]
        for r in range(0, VOX, 64):
            g = iv * (ngrad[i, r : r + 64, :] - m1 - conv[i, r : r + 64, :] * m2)
            cgrad[i, r : r + 64, :] = g.astype(BF16)
        return c

    lax.fori_loop(0, WSLOTS, conv_gradient, 0)

    share = ROWS // chips

    batches = [(0, 8), (8, 16), (16, 22), (22, 27)]

    def mate_copy(b):
        lo, hi = batches[b]
        rows = pl.ds(lo * C_IN, (hi - lo) * C_IN)
        return remote(half.at[1 - core, rows], other.at[rows], c_send.at[b], c_recv.at[b], tile=mate)

    row, col = lax.div(chip, SIDE), lax.rem(chip, SIDE)
    u = col + core * (row - col)
    v = row + core * (col - row)

    def chip_at(pu, pv):
        return pu * (1 + (SIDE - 1) * core) + pv * (SIDE - (SIDE - 1) * core)

    def place(j):
        return j % SIDE + core * (j // SIDE - j % SIDE), j // SIDE + core * (j % SIDE - j // SIDE)

    def ring_copy(j, slot, pu, pv):
        to = chip_at(pu, v) * 2 + core
        at = slot * SIDE + pv
        return remote(half.at[core, pl.ds(j * share, share)], part.at[at], p_send.at[j], p_recv.at[at], tile=to)

    def cross_copy(slot, pv):
        to = chip_at(u, pv) * 2 + core
        return remote(ring.at[pv], part2.at[slot], r_send.at[pv], r_recv.at[slot], tile=to)

    done = [0]

    def settle(b):
        lo, hi = batches[b][0] * C_IN, batches[b][1] * C_IN
        mate_copy(b).wait_recv()
        half[core, lo:hi, :] = half[core, lo:hi, :] + other[lo:hi, :]
        while (done[0] + 1) * share <= hi:
            j = done[0]

            pu, pv = place(j)

            @pl.when(pu != u)
            def _():
                ring_copy(j, u, pu, pv).start()

            @pl.when(pu == u)
            def _():
                part[u * SIDE + pv] = half[core, j * share : (j + 1) * share, :]

            done[0] += 1

    for b, (first_tap, end_tap) in enumerate(batches):
        for p in range(first_tap, end_tap, 2):
            d = None
            for n in range(0, WSLOTS, 4):
                rows = jnp.concatenate([pair_slab(even, odd, i, p) for i in range(n, n + 4)], axis=0)
                g = jnp.concatenate([cgrad[i] for i in range(n, n + 4)], axis=0)
                t = lax.dot_general(rows, g, (((0,), (0,)), ((), ())), preferred_element_type=F32)
                d = t if d is None else d + t
            lo, hi = p * C_IN, min(p + 2, 27) * C_IN
            half[0, lo:hi, :] = d[:, :128]
            half[1, lo:hi, :] = d[:, 128:]
        mate_copy(b).start()
        if b > 0:
            settle(b - 1)
    settle(len(batches) - 1)

    def ring_sum(s, c):
        pv = lax.rem(v + s, SIDE)
        for t in range(1, SIDE):
            pu = lax.rem(u + t, SIDE)
            ring_copy(0, pu, pu, pv).wait_recv()
        ring[pv] = sum(part[pu * SIDE + pv] for pu in range(SIDE))

        @pl.when(pv != v)
        def _():
            cross_copy(v, pv).start()

        @pl.when(pv == v)
        def _():
            part2[v] = ring[v]

        return c

    lax.fori_loop(1, SIDE + 1, ring_sum, 0)
    for j in range(chips):
        pu, pv = place(j)

        @pl.when(pu != u)
        def _():
            ring_copy(j, u, pu, pv).wait_send()

    for b in range(len(batches)):
        mate_copy(b).wait_send()

    def cross_wait(s, c):
        pv = lax.rem(v + s, SIDE)
        cross_copy(v, pv).wait_send()
        cross_copy(pv, pv).wait_recv()
        return c

    lax.fori_loop(1, SIDE, cross_wait, 0)

    piece = red.shape[0] // n_rep
    red[0:share, :] = jnp.sum(part2[...], axis=0)
    if red.shape[0] > share:
        red[share:, :] = jnp.zeros((red.shape[0] - share, 128), F32)
    zin[rep] = red[pl.ds(pl.multiple_of(rep * piece, 8), piece), :]

    def z_copy(to, slot, s):
        return remote(red.at[pl.ds(pl.multiple_of(to * piece, 8), piece)], zin.at[slot], z_send.at[s], z_recv.at[slot], rep=to)

    def rows_at(r):
        return pl.ds(pl.multiple_of(r * piece, 8), piece)

    def y_copy(side, to, slot, s):
        tile = me if side == 0 else mate
        from_core = core if side == 0 else 1 - core
        mine = zout.at[core, rows_at(rep)]
        there = zout.at[core, rows_at(rep)] if slot is None else zout.at[from_core, rows_at(slot)]
        got = core * n_rep + rep if slot is None else from_core * n_rep + slot
        return remote(mine, there, y_send.at[side * n_rep + s], y_recv.at[got], tile=tile, rep=to)

    def each(what):
        def body(s, c):
            what(lax.rem(rep + s, n_rep), s)
            return c

        lax.fori_loop(1, n_rep, body, 0)

    each(lambda to, s: z_copy(to, rep, s).start())
    lax.fori_loop(1, n_rep, norm_wait, 0)
    norm[...] = jnp.sum(nbuf[...], axis=0)
    each(lambda to, s: z_copy(to, rep, s).wait_send())
    each(lambda to, s: z_copy(to, to, s).wait_recv())
    zout[core, rows_at(rep), :] = jnp.sum(zin[...], axis=0)
    y_copy(1, rep, None, 0).start()
    for side in range(2):
        each(lambda to, s: y_copy(side, to, None, s).start())
    y_copy(1, rep, None, 0).wait_send()
    y_copy(1, rep, rep, 0).wait_recv()
    for side in range(2):
        each(lambda to, s: y_copy(side, to, None, s).wait_send())
        each(lambda to, s: y_copy(side, to, to, s).wait_recv())

    keep = grad.shape[0]
    own = pl.ds(pl.multiple_of(core * (share - keep), 8), keep)
    grad[:, 0:128] = zout[0, own, :]
    grad[:, 128:256] = zout[1, own, :]


def main_call(n_tile, n_rep, strip, mine, meta, filt, up, clips, gains, shifts):
    lines = n_tile * TH
    depth = lines // RMOD + 2
    chips = n_tile // 2
    share = ROWS // chips
    keep = share // 2 + 4 if (share // 2) % 8 else share // 2
    padded = -(-share // (8 * n_rep)) * 8 * n_rep
    whole = pl.BlockSpec(memory_space=pltpu.VMEM)
    hbm = pl.BlockSpec(memory_space=pl.ANY)
    dma = pltpu.SemaphoreType.DMA
    return pl.pallas_call(
        partial(main_kernel, n_tile, n_rep),
        out_shape=(
            jax.ShapeDtypeStruct((WSLOTS, VOX, C_OUT), BF16),
            jax.ShapeDtypeStruct((keep, C_OUT), F32),
            jax.ShapeDtypeStruct((8, 128), F32),
        ),
        in_specs=[hbm, whole, pl.BlockSpec(memory_space=pltpu.SMEM), hbm, hbm, whole, whole, whole],
        out_specs=(whole,) * 3,
        scratch_shapes=[
            pltpu.VMEM((ROWS, C_OUT), BF16),
            pltpu.VMEM((WSLOTS, VOX, C_OUT), BF16),
            pltpu.VMEM((CLIPS, WSLOTS, C_OUT), F32),
            dma((2,)),
            pltpu.VMEM((3, WSLOTS, 480, C_IN), BF16),
            pltpu.VMEM((3, WSLOTS, 384, C_IN), BF16),
            pltpu.VMEM((WSLOTS, VOX, C_OUT), F32),
            pltpu.VMEM((WSLOTS, VOX, C_OUT), F32),
            pltpu.VMEM((WSLOTS, VOX, C_OUT), BF16),
            pltpu.VMEM((WSLOTS, C_OUT), F32),
            pltpu.VMEM((WSLOTS, C_OUT), F32),
            pltpu.VMEM((WSLOTS, C_OUT), F32),
            pltpu.VMEM((WSLOTS, C_OUT), F32),
            pltpu.VMEM((8, 128), F32),
            pltpu.VMEM((n_tile, 8, 128), F32),
            pltpu.VMEM((2, ROWS, 128), F32),
            pltpu.VMEM((ROWS, 128), F32),
            pltpu.VMEM((chips, share, 128), F32),
            pltpu.VMEM((SIDE, share, 128), F32),
            pltpu.VMEM((SIDE, share, 128), F32),
            pltpu.VMEM((padded, 128), F32),
            pltpu.VMEM((n_rep, padded // n_rep, 128), F32),
            pltpu.VMEM((2, padded, 128), F32),
            pltpu.VMEM((n_rep, 8, 128), F32),
            pltpu.VMEM((8, 128), F32),
            pltpu.VMEM((n_tile, 8, 128), F32),
        ]
        + [dma((n_tile,))] * 4
        + [dma((14,))] * 2
        + [dma((chips,))] * 2
        + [dma((SIDE,))] * 2
        + [dma((n_rep,))] * 2
        + [dma((2 * n_rep,))] * 2
        + [dma((n_rep,))] * 2
        + [
            pltpu.VMEM((n_tile, 1, 128), jnp.int32),
            pltpu.SMEM((n_tile, 1, 128), jnp.int32),
            pltpu.VMEM((PLANES, lines // RMOD + 1, 8 * WBLK, C_IN), BF16),
            pltpu.VMEM(((PLANES + 1) * depth, WBLK + 1, 8, C_IN), F32),
            pltpu.VMEM((PART * PIECE, C_IN), F32),
            pltpu.VMEM((n_tile * PARTS, PART * PIECE, C_IN), BF16),
            pltpu.VMEM((STOPS * PARTS, PART * PIECE, C_IN), BF16),
            pltpu.VMEM((STOPS * 2 * PART, 16, C_IN), F32),
            dma((n_tile,)),
            dma((n_tile,)),
            dma,
            dma((TH * FMOD,)),
            dma((lines // RMOD + 1,)),
            dma((TH,)),
            dma((n_tile * PARTS,)),
            dma((STOPS * PARTS,)),
        ],
        compiler_params=pltpu.CompilerParams(collective_id=0, has_side_effects=True, vmem_limit_bytes=VMEM_BYTES),
        cost_estimate=pl.CostEstimate(flops=4 * WSLOTS * VOX * ROWS * C_OUT, bytes_accessed=16 * 1024 * 1024, transcendentals=WSLOTS * VOX * C_OUT),
        name="conv_norm",
    )(strip, mine, meta, filt, up, clips, gains, shifts)


def shards(
    input_video,
    block_clip,
    send_slot,
    recv_index,
    tile_clip,
    kernel,
    norm_gain,
    norm_shift,
    upstream,
):
    peer_count = lax.axis_size("tile")
    me = lax.axis_index("tile")
    strip = input_video[0].reshape(PLANES, FMOD, TH, 8 * WBLK, C_IN)
    clip_ids = block_clip[0]
    mine = jnp.concatenate(
        [send_slot[0, 0].reshape(-1), recv_index[0, 0], jnp.zeros((128 - 2 * peer_count - WSLOTS,), jnp.int32)]
    )[None]
    depth = peer_count * TH // RMOD + 2
    block = jnp.arange(TBLK, dtype=jnp.int32)
    place = (me % FMOD - TT * block + 2) % FMOD
    linked = jnp.concatenate([jnp.zeros((1,), bool), clip_ids[1:] == clip_ids[:-1]])
    plane = jnp.where((place >= 2) | linked, (TT * block - 2 + place) // FMOD, PLANES)
    owner = jnp.arange(peer_count, dtype=jnp.int32)
    top = owner * TH - 1
    line = (top + (me // FMOD - top) % RMOD - me // FMOD + RMOD) // RMOD
    meta = jnp.concatenate(
        [plane * depth, jnp.zeros((2,), jnp.int32), line, jnp.zeros((120 - peer_count,), jnp.int32)]
    )[None]
    activation, grad_rows, norm_rows = main_call(
        peer_count, lax.axis_size("rep"), strip, mine, meta, kernel, upstream[0, 0],
        tile_clip[0, 0][:, None], norm_gain[None], norm_shift[None]
    )
    row_share = ROWS // peer_count
    skip = (grad_rows.shape[0] - row_share) * lax.rem(lax.axis_index("tile"), 2)
    grad_shard = lax.dynamic_slice_in_dim(grad_rows, skip, row_share, 0)
    return (activation[None, None], grad_shard, norm_rows[2:6].reshape(2, C_OUT))


def solution(mesh):
    placed = (
        P("rep", None, "tile", None, None),
        P("rep", None),
        P("rep", "tile", None, None),
        P("rep", "tile", None),
        P("rep", "tile", None),
        P(),
        P(),
        P(),
        P("rep", "tile", None, None, None),
    )
    return jax.shard_map(
        shards,
        mesh=mesh,
        in_specs=placed,
        out_specs=(P("rep", "tile", None, None, None), P("tile", None), P()),
        check_vma=False,
    )
```

```python
from functools import partial

import jax
import jax.numpy as jnp
from jax import lax
from jax.experimental import pallas as pl
from jax.experimental.pallas import tpu as pltpu
from jax.sharding import PartitionSpec as P

C_IN = 128
C_OUT = 256
GROUPS = 32
CPG = 8
TT = 4
TH = 8
TW = 8
TBLK = 6
CLIPS = 3
WBLK = 8
WSLOTS = 16
VOX = 256
FRAMES = 24


epsilon = 1e-05


MESH = pl.DeviceIdType.MESH
TAP = [(a, e, q) for a in range(3) for e in range(3) for q in range(3)]
F32, BF16 = jnp.float32, jnp.bfloat16
ROWS = 27 * C_IN
SIDE = 4
GVOX = float(VOX * CPG)
SLAB = 60 * 8
VMEM_BYTES = 60 * 1024 * 1024


def remote(src, dst, send, recv, **where):
    return pltpu.make_async_remote_copy(
        src_ref=src, dst_ref=dst, send_sem=send, recv_sem=recv, device_id=where, device_id_type=MESH
    )


def gather_block(block, buf, send, recv, me, count):
    buf[me] = block[...]

    def start(s, c):
        to = lax.rem(me + s, count)
        remote(block, buf.at[me], send.at[s], recv.at[me], tile=to).start()
        return c

    def wait(s, c):
        to = lax.rem(me + s, count)
        remote(block, buf.at[me], send.at[s], recv.at[to], tile=to).wait_send()
        remote(block, buf.at[to], send.at[s], recv.at[to], tile=to).wait_recv()
        return c

    lax.fori_loop(1, count, start, 0)
    lax.fori_loop(1, count, wait, 0)


def shifted(i, x, even, odd):
    for q in range(3):
        y = x[:, :, q : q + 8, :]
        even[q, i] = y.reshape(480, C_IN).astype(BF16)
        odd[q, i] = y[:, 1:9].reshape(384, C_IN).astype(BF16)


def tap_slab(even, odd, i, tap):
    a, e, q = tap
    out = []
    for f in range(TT):
        if e == 1:
            out.append(odd[q, i, pl.ds((f + a) * 64, 64), :])
        else:
            out.append(even[q, i, pl.ds((f + a) * 80 + e * 8, 64), :])
    return jnp.concatenate(out, axis=0)


def pair_slab(even, odd, i, p):
    left = tap_slab(even, odd, i, TAP[p])
    if p + 1 == len(TAP):
        return left
    return jnp.concatenate([left, tap_slab(even, odd, i, TAP[p + 1])], axis=1)


FMOD = 6
RMOD = 5
STOPS = FMOD * RMOD
PIECE = 20
PARTS = 2
PART = WSLOTS // PARTS
PLANES = FRAMES // FMOD


def ordered_peer(me, s):
    core, chip = lax.rem(me, 2), lax.div(me, 2)
    row, col = lax.div(chip, SIDE), lax.rem(chip, SIDE)
    n = lax.div(s, 2)
    p, q = lax.rem(n, SIDE), lax.rem(n + lax.div(n, SIDE), SIDE)
    x = lax.rem(col + p + core * (q - p), SIDE)
    y = lax.rem(row + q + core * (p - q), SIDE)
    return (y * SIDE + x) * 2 + lax.rem(core + lax.rem(s, 2), 2)


def exchange(
    n_tile, me, greeted, strip, mine, meta,
    tab, stab, raw, wide, stage, sendb, recvb, rows32,
    t_send, t_recv, s_sem, v_send, v_recv, v_own, w_send, w_recv,
):
    lines = n_tile * TH
    my_f = lax.rem(me, FMOD)
    my_r = lax.div(me, FMOD)
    depth = lines // RMOD + 2
    tab[me] = mine[...]
    greeted()

    def table(to, slot, s):
        return remote(mine, tab.at[slot], t_send.at[s], t_recv.at[slot], tile=to)

    def table_start(s, c):
        table(lax.rem(me + s, n_tile), me, s).start()
        return c

    def table_wait(s, c):
        to = lax.rem(me + s, n_tile)
        table(to, me, s).wait_send()
        table(to, to, s).wait_recv()
        return c

    lax.fori_loop(1, n_tile, table_start, 0)

    def lines_to(to, what):
        a = lax.rem(to, FMOD)
        h0 = lax.rem(lax.div(to, FMOD) + RMOD * TH - lax.rem(me * TH, RMOD), RMOD)

        @pl.when(to < STOPS)
        def _():
            what(a, h0, lax.div(me * TH + h0, RMOD))

            @pl.when(h0 < TH - RMOD)
            def _():
                what(a, h0 + RMOD, lax.div(me * TH + h0 + RMOD, RMOD))

    def line_copy(to, a, h, index):
        return remote(strip.at[:, a, h], raw.at[:, index], v_send.at[h * FMOD + a], v_recv.at[index], tile=to)

    def spread(s, c):
        to = ordered_peer(me, s)
        lines_to(to, lambda a, h, index: line_copy(to, a, h, index).start())
        return c

    def keep(a, h, index):
        pltpu.make_async_copy(strip.at[:, a, h], raw.at[:, index], v_own.at[h]).start()

    lax.fori_loop(1, n_tile, spread, 0)
    lines_to(me, keep)

    def clear(i, c):
        wide[i] = jnp.zeros(wide.shape[1:], F32)
        return c

    lax.fori_loop(0, wide.shape[0], clear, 0)

    lax.fori_loop(1, n_tile, table_wait, 0)
    scalars = pltpu.make_async_copy(tab, stab, s_sem)
    scalars.start()

    @pl.when(me < STOPS)
    def _():
        def arrive(i, c):
            y = i * RMOD + my_r
            owner = lax.div(y, TH)
            h = lax.rem(y, TH)

            @pl.when(owner != me)
            def _():
                remote(strip.at[:, my_f, h], raw.at[:, i], v_send.at[0], v_recv.at[i], tile=owner).wait_recv()

            @pl.when(owner == me)
            def _():
                pltpu.make_async_copy(strip.at[:, my_f, h], raw.at[:, i], v_own.at[h]).wait()

            for k in range(PLANES):
                line = raw[k, i].astype(F32)
                gap = jnp.zeros((1, C_IN), F32)
                line = jnp.concatenate([gap, line, gap, jnp.zeros((6, C_IN), F32)], axis=0)
                wide[k * depth + i + 1] = line.reshape(WBLK + 1, 8, C_IN)
            return c

        lax.fori_loop(0, lax.div(lines - my_r + RMOD - 1, RMOD), arrive, 0)

    scalars.wait()

    def part_copy(w, slot, h):
        return remote(sendb.at[w * PARTS + h], recvb.at[slot * PARTS + h], w_send.at[w * PARTS + h], w_recv.at[slot * PARTS + h], tile=w)

    @pl.when(me < STOPS)
    def _():
        def serve(step, c):
            h = lax.div(step, n_tile)
            w = ordered_peer(me, lax.rem(step + 1, n_tile))
            for j in range(PART):
                r = stab[w, 0, 64 + h * PART + j]
                t = lax.div(r, 2)
                slot = stab[t, 0, w * 2 + lax.rem(r, 2)]
                base = meta[0, lax.div(slot, WBLK)] + meta[0, 8 + t]
                first = lax.rem(slot, WBLK)
                for half in range(2):
                    at = j * PIECE + half * 10
                    stage[at : at + 8, :] = wide[base + half, first]
                    stage[at + 8 : at + 10, :] = wide[base + half, first + 1][:2]
            sendb[w * PARTS + h] = stage[...].astype(BF16)

            @pl.when(w != me)
            def _():
                part_copy(w, me, h).start()

            @pl.when(w == me)
            def _():
                recvb[me * PARTS + h] = sendb[me * PARTS + h]

            return c

        lax.fori_loop(0, PARTS * n_tile, serve, 0)

    def land(h):
        def body(s, c):
            i = ordered_peer(me, lax.rem(s, n_tile))

            @pl.when(i < STOPS)
            def _():
                @pl.when(i != me)
                def _():
                    part_copy(i, i, h).wait_recv()

                v = recvb[i * PARTS + h].astype(F32)
                for j in range(PART):
                    for half in range(2):
                        at = j * PIECE + half * 10
                        rows32[i * 2 * PART + j * 2 + half, 0:10, :] = v[at : at + 10]

            return c

        lax.fori_loop(1, n_tile + 1, body, 0)

    def tile_rows(h, j):
        r = stab[me, 0, 64 + h * PART + j]
        t = lax.div(r, 2)
        b = lax.div(stab[t, 0, me * 2 + lax.rem(r, 2)], WBLK)
        out = []
        for f in range(TT + 2):
            a = lax.rem(b * TT + TT + f, FMOD)
            for y in range(TH + 2):
                q = lax.rem(t * TH + 4 + y % RMOD, RMOD)
                at = (q * FMOD + a) * (2 * PART) + j * 2 + y // RMOD
                out.append(rows32[at, 0:10, :])
        return jnp.stack(out, axis=0).reshape(TT + 2, TH + 2, TW + 2, C_IN)

    def drain():
        def sent(s, c):
            to = ordered_peer(me, s)
            lines_to(to, lambda a, h, index: line_copy(to, a, h, index).wait_send())
            return c

        lax.fori_loop(1, n_tile, sent, 0)

        @pl.when(me < STOPS)
        def _():
            def served(s, c):
                w = lax.rem(me + s, n_tile)
                for h in range(PARTS):
                    part_copy(w, me, h).wait_send()
                return c

            lax.fori_loop(1, n_tile, served, 0)

    return land, tile_rows, drain


def main_kernel(
    n_tile, n_rep, strip, mine, meta, filt_hbm, up_hbm, clips, gains, shifts, act, grad, norm,
    filt, up, member, load_sem, even, odd, conv, ngrad, cgrad, sums, sq, tmean, tinv, blk, buf, half, other, part, ring, part2, red, zin, zout, nbuf, blk2, buf2,
    g_send, g_recv, h_send, h_recv, c_send, c_recv, p_send, p_recv, r_send, r_recv, z_send, z_recv, y_send, y_recv, n_send, n_recv, *moving,
):
    me = lax.axis_index("tile")
    rep = lax.axis_index("rep")
    core = lax.rem(me, 2)
    chip = lax.div(me, 2)
    chips = n_tile // 2
    mate = chip * 2 + 1 - core
    loss_scale = float(n_rep * n_tile * WSLOTS * VOX) ** (-0.5)

    barrier = pltpu.get_barrier_semaphore()

    def greet_tile(s, c):
        pl.semaphore_signal(barrier, inc=1, device_id={"tile": lax.rem(me + s, n_tile)}, device_id_type=MESH)
        return c

    def greet_rep(s, c):
        pl.semaphore_signal(barrier, inc=1, device_id={"rep": lax.rem(rep + s, n_rep)}, device_id_type=MESH)
        return c

    def greet_mate(s, c):
        where = {"tile": mate, "rep": lax.rem(rep + s, n_rep)}
        pl.semaphore_signal(barrier, inc=1, device_id=where, device_id_type=MESH)
        return c

    lax.fori_loop(1, n_tile, greet_tile, 0)
    lax.fori_loop(1, n_rep, greet_rep, 0)
    lax.fori_loop(1, n_rep, greet_mate, 0)

    gi = lax.broadcasted_iota(jnp.int32, (C_OUT, C_OUT), 0) >> 3
    gj = lax.broadcasted_iota(jnp.int32, (C_OUT, C_OUT), 1) >> 3
    same_group = (gi == gj).astype(F32)

    def exact(v, w):
        return jnp.dot(v, w, precision=lax.Precision.HIGHEST, preferred_element_type=F32)

    def per_group(v):
        return exact(v, same_group)

    def packed(rows):
        ch = lax.broadcasted_iota(jnp.int32, (C_OUT, 128), 0) >> 3
        lane = lax.broadcasted_iota(jnp.int32, (C_OUT, 128), 1)
        return sum(exact(rows[k], (lane == ch + k * GROUPS).astype(F32)) for k in range(CLIPS))

    def unpacked(v, k):
        lane = lax.broadcasted_iota(jnp.int32, (128, C_OUT), 0)
        ch = lax.broadcasted_iota(jnp.int32, (128, C_OUT), 1) >> 3
        return exact(v, (lane == ch + k * GROUPS).astype(F32))

    def greeted():
        pl.semaphore_wait(barrier, n_tile + 2 * n_rep - 3)

    load_filt = pltpu.make_async_copy(filt_hbm, filt, load_sem.at[0])
    load_up = pltpu.make_async_copy(up_hbm, up, load_sem.at[1])
    load_filt.start()
    load_up.start()
    for k in range(CLIPS):
        member[k] = jnp.broadcast_to((clips[...] == k).astype(F32), (WSLOTS, C_OUT))

    land, tile_rows, drain = exchange(n_tile, me, greeted, strip, mine, meta, *moving)

    def forward(n, c):
        acc = None
        for p in range(0, 27, 2):
            rows = jnp.concatenate([pair_slab(even, odd, n * 4 + j, p) for j in range(4)], axis=0)
            d = jnp.dot(rows, filt[p * C_IN : min(p + 2, 27) * C_IN, :], preferred_element_type=F32)
            acc = d if acc is None else acc + d
        for j in range(4):
            one = acc[j * VOX : (j + 1) * VOX]
            conv[n * 4 + j] = one
            sums[pl.ds(n * 4 + j, 1), :] = jnp.sum(one, axis=0, keepdims=True)
        return c

    load_filt.wait()
    load_up.wait()
    for h in range(PARTS):
        land(h)

        def unpack(j, c):
            shifted(h * PART + j, tile_rows(h, j), even, odd)
            return c

        lax.fori_loop(0, PART, unpack, 0)
        lax.fori_loop(h * PART // 4, (h + 1) * PART // 4, forward, 0)

    gsum = per_group(sums[...])
    tmean[...] = gsum / GVOX

    def centre(i, c):
        d = conv[i] - tmean[pl.ds(i, 1), :]
        sq[pl.ds(i, 1), :] = jnp.sum(d * d, axis=0, keepdims=True)
        return c

    lax.fori_loop(0, WSLOTS, centre, 0)
    local = []
    for k in range(CLIPS):
        m = member[k]
        n_k = jnp.sum(m, axis=0, keepdims=True)
        mu = jnp.sum(m * gsum, axis=0, keepdims=True) / (GVOX * jnp.maximum(n_k, 1.0))
        off = tmean[...] - mu
        first = jnp.sum(m * sums[...], axis=0, keepdims=True)
        second = jnp.sum(m * (sq[...] + float(VOX) * off * off), axis=0, keepdims=True)
        local.append(jnp.concatenate([n_k / float(CPG), first, second, jnp.zeros((5, C_OUT), F32)], axis=0))
    blk[...] = packed(local)

    gather_block(blk, buf, g_send, g_recv, me, n_tile)

    all_n = buf[:, 0:1, :]
    all_s = buf[:, 1:2, :]
    n_tot = jnp.maximum(jnp.sum(all_n, axis=0), 1.0)
    mean = jnp.sum(all_s, axis=0) / (GVOX * n_tot)
    off = all_s / (GVOX * jnp.maximum(all_n, 1.0)) - mean
    var = jnp.sum(buf[:, 2:3, :] + GVOX * all_n * off * off, axis=0) / (GVOX * n_tot)
    table = jnp.concatenate([mean, lax.rsqrt(var + epsilon), jnp.zeros((6, 128), F32)], axis=0)
    wide_table = [unpacked(table, k) for k in range(CLIPS)]
    tmean[...] = sum(member[k] * wide_table[k][0:1] for k in range(CLIPS))
    tinv[...] = sum(member[k] * wide_table[k][1:2] for k in range(CLIPS))

    gain = gains[...]
    shift = shifts[...]

    def middle(i, c):
        mu = tmean[pl.ds(i, 1), :]
        iv = tinv[pl.ds(i, 1), :]
        first = jnp.zeros((1, C_OUT), F32)
        cross = jnp.zeros((1, C_OUT), F32)
        for r in range(0, VOX, 64):
            normed = (conv[i, r : r + 64, :] - mu) * iv
            pre = normed * gain + shift
            sg = 1.0 / (1.0 + jnp.exp(-pre))
            act[i, r : r + 64, :] = (pre * sg).astype(BF16)
            pg = (up[i, r : r + 64, :].astype(F32) * loss_scale) * sg * (1.0 + pre * (1.0 - sg))
            first += jnp.sum(pg, axis=0, keepdims=True)
            cross += jnp.sum(pg * normed, axis=0, keepdims=True)
            conv[i, r : r + 64, :] = normed
            ngrad[i, r : r + 64, :] = pg * gain
        sums[pl.ds(i, 1), :] = first
        sq[pl.ds(i, 1), :] = cross
        return c

    lax.fori_loop(0, WSLOTS, middle, 0)
    firsts = [jnp.sum(member[k] * sums[...], axis=0, keepdims=True) for k in range(CLIPS)]
    crosses = [jnp.sum(member[k] * sq[...], axis=0, keepdims=True) for k in range(CLIPS)]
    zeros = jnp.zeros((6, C_OUT), F32)
    scaled = packed([jnp.concatenate([firsts[k] * gain, crosses[k] * gain, zeros], axis=0) for k in range(CLIPS)])
    over_clips = [sum(crosses), sum(firsts)]
    halves = [v[:, lo : lo + 128] for v in over_clips for lo in (0, 128)]
    blk2[...] = jnp.concatenate([scaled[0:2]] + halves + [jnp.zeros((2, 128), F32)], axis=0)
    gather_block(blk2, buf2, h_send, h_recv, me, n_tile)
    total = jnp.sum(buf2[...], axis=0)

    nbuf[rep] = total

    def norm_start(s, c):
        to = lax.rem(rep + s, n_rep)
        remote(nbuf.at[rep], nbuf.at[rep], n_send.at[s], n_recv.at[rep], rep=to).start()
        return c

    def norm_wait(s, c):
        to = lax.rem(rep + s, n_rep)
        remote(nbuf.at[rep], nbuf.at[rep], n_send.at[s], n_recv.at[to], rep=to).wait_send()
        remote(nbuf.at[rep], nbuf.at[to], n_send.at[s], n_recv.at[to], rep=to).wait_recv()
        return c

    lax.fori_loop(1, n_rep, norm_start, 0)

    table = total / (GVOX * n_tot)
    wide_table = [unpacked(table, k) for k in range(CLIPS)]
    sums[...] = sum(member[k] * wide_table[k][0:1] for k in range(CLIPS))
    sq[...] = sum(member[k] * wide_table[k][1:2] for k in range(CLIPS))

    def conv_gradient(i, c):
        iv = tinv[pl.ds(i, 1), :]
        m1 = sums[pl.ds(i, 1), :]
        m2 = sq[pl.ds(i, 1), :]
        for r in range(0, VOX, 64):
            g = iv * (ngrad[i, r : r + 64, :] - m1 - conv[i, r : r + 64, :] * m2)
            cgrad[i, r : r + 64, :] = g.astype(BF16)
        return c

    lax.fori_loop(0, WSLOTS, conv_gradient, 0)

    share = ROWS // chips

    batches = [(0, 8), (8, 16), (16, 22), (22, 27)]

    def mate_copy(b):
        lo, hi = batches[b]
        rows = pl.ds(lo * C_IN, (hi - lo) * C_IN)
        return remote(half.at[1 - core, rows], other.at[rows], c_send.at[b], c_recv.at[b], tile=mate)

    row, col = lax.div(chip, SIDE), lax.rem(chip, SIDE)
    u = col + core * (row - col)
    v = row + core * (col - row)

    def chip_at(pu, pv):
        return pu * (1 + (SIDE - 1) * core) + pv * (SIDE - (SIDE - 1) * core)

    def place(j):
        return j % SIDE + core * (j // SIDE - j % SIDE), j // SIDE + core * (j % SIDE - j // SIDE)

    def ring_copy(j, slot, pu, pv):
        to = chip_at(pu, v) * 2 + core
        at = slot * SIDE + pv
        return remote(half.at[core, pl.ds(j * share, share)], part.at[at], p_send.at[j], p_recv.at[at], tile=to)

    def cross_copy(slot, pv):
        to = chip_at(u, pv) * 2 + core
        return remote(ring.at[pv], part2.at[slot], r_send.at[pv], r_recv.at[slot], tile=to)

    done = [0]

    def settle(b):
        lo, hi = batches[b][0] * C_IN, batches[b][1] * C_IN
        mate_copy(b).wait_recv()
        half[core, lo:hi, :] = half[core, lo:hi, :] + other[lo:hi, :]
        while (done[0] + 1) * share <= hi:
            j = done[0]

            pu, pv = place(j)

            @pl.when(pu != u)
            def _():
                ring_copy(j, u, pu, pv).start()

            @pl.when(pu == u)
            def _():
                part[u * SIDE + pv] = half[core, j * share : (j + 1) * share, :]

            done[0] += 1

    for b, (first_tap, end_tap) in enumerate(batches):
        for p in range(first_tap, end_tap, 2):
            d = None
            for n in range(0, WSLOTS, 4):
                rows = jnp.concatenate([pair_slab(even, odd, i, p) for i in range(n, n + 4)], axis=0)
                g = jnp.concatenate([cgrad[i] for i in range(n, n + 4)], axis=0)
                t = lax.dot_general(rows, g, (((0,), (0,)), ((), ())), preferred_element_type=F32)
                d = t if d is None else d + t
            lo, hi = p * C_IN, min(p + 2, 27) * C_IN
            half[0, lo:hi, :] = d[:, :128]
            half[1, lo:hi, :] = d[:, 128:]
        mate_copy(b).start()
        if b > 0:
            settle(b - 1)
    settle(len(batches) - 1)

    def ring_sum(s, c):
        pv = lax.rem(v + s, SIDE)
        for t in range(1, SIDE):
            pu = lax.rem(u + t, SIDE)
            ring_copy(0, pu, pu, pv).wait_recv()
        ring[pv] = sum(part[pu * SIDE + pv] for pu in range(SIDE))

        @pl.when(pv != v)
        def _():
            cross_copy(v, pv).start()

        @pl.when(pv == v)
        def _():
            part2[v] = ring[v]

        return c

    drain()
    lax.fori_loop(1, SIDE + 1, ring_sum, 0)
    for j in range(chips):
        pu, pv = place(j)

        @pl.when(pu != u)
        def _():
            ring_copy(j, u, pu, pv).wait_send()

    for b in range(len(batches)):
        mate_copy(b).wait_send()

    def cross_wait(s, c):
        pv = lax.rem(v + s, SIDE)
        cross_copy(v, pv).wait_send()
        cross_copy(pv, pv).wait_recv()
        return c

    lax.fori_loop(1, SIDE, cross_wait, 0)

    piece = red.shape[0] // n_rep
    red[0:share, :] = jnp.sum(part2[...], axis=0)
    if red.shape[0] > share:
        red[share:, :] = jnp.zeros((red.shape[0] - share, 128), F32)
    zin[rep] = red[pl.ds(pl.multiple_of(rep * piece, 8), piece), :]

    def z_copy(to, slot, s):
        return remote(red.at[pl.ds(pl.multiple_of(to * piece, 8), piece)], zin.at[slot], z_send.at[s], z_recv.at[slot], rep=to)

    def rows_at(r):
        return pl.ds(pl.multiple_of(r * piece, 8), piece)

    def y_copy(side, to, slot, s):
        tile = me if side == 0 else mate
        from_core = core if side == 0 else 1 - core
        mine = zout.at[core, rows_at(rep)]
        there = zout.at[core, rows_at(rep)] if slot is None else zout.at[from_core, rows_at(slot)]
        got = core * n_rep + rep if slot is None else from_core * n_rep + slot
        return remote(mine, there, y_send.at[side * n_rep + s], y_recv.at[got], tile=tile, rep=to)

    def each(what):
        def body(s, c):
            what(lax.rem(rep + s, n_rep), s)
            return c

        lax.fori_loop(1, n_rep, body, 0)

    each(lambda to, s: z_copy(to, rep, s).start())
    lax.fori_loop(1, n_rep, norm_wait, 0)
    norm[...] = jnp.sum(nbuf[...], axis=0)
    each(lambda to, s: z_copy(to, rep, s).wait_send())
    each(lambda to, s: z_copy(to, to, s).wait_recv())
    zout[core, rows_at(rep), :] = jnp.sum(zin[...], axis=0)
    y_copy(1, rep, None, 0).start()
    for side in range(2):
        each(lambda to, s: y_copy(side, to, None, s).start())
    y_copy(1, rep, None, 0).wait_send()
    y_copy(1, rep, rep, 0).wait_recv()
    for side in range(2):
        each(lambda to, s: y_copy(side, to, None, s).wait_send())
        each(lambda to, s: y_copy(side, to, to, s).wait_recv())

    keep = grad.shape[0]
    own = pl.ds(pl.multiple_of(core * (share - keep), 8), keep)
    grad[:, 0:128] = zout[0, own, :]
    grad[:, 128:256] = zout[1, own, :]


def main_call(n_tile, n_rep, strip, mine, meta, filt, up, clips, gains, shifts):
    lines = n_tile * TH
    depth = lines // RMOD + 2
    chips = n_tile // 2
    share = ROWS // chips
    keep = share // 2 + 4 if (share // 2) % 8 else share // 2
    padded = -(-share // (8 * n_rep)) * 8 * n_rep
    whole = pl.BlockSpec(memory_space=pltpu.VMEM)
    hbm = pl.BlockSpec(memory_space=pl.ANY)
    dma = pltpu.SemaphoreType.DMA
    return pl.pallas_call(
        partial(main_kernel, n_tile, n_rep),
        out_shape=(
            jax.ShapeDtypeStruct((WSLOTS, VOX, C_OUT), BF16),
            jax.ShapeDtypeStruct((keep, C_OUT), F32),
            jax.ShapeDtypeStruct((8, 128), F32),
        ),
        in_specs=[hbm, whole, pl.BlockSpec(memory_space=pltpu.SMEM), hbm, hbm, whole, whole, whole],
        out_specs=(whole,) * 3,
        scratch_shapes=[
            pltpu.VMEM((ROWS, C_OUT), BF16),
            pltpu.VMEM((WSLOTS, VOX, C_OUT), BF16),
            pltpu.VMEM((CLIPS, WSLOTS, C_OUT), F32),
            dma((2,)),
            pltpu.VMEM((3, WSLOTS, 480, C_IN), BF16),
            pltpu.VMEM((3, WSLOTS, 384, C_IN), BF16),
            pltpu.VMEM((WSLOTS, VOX, C_OUT), F32),
            pltpu.VMEM((WSLOTS, VOX, C_OUT), F32),
            pltpu.VMEM((WSLOTS, VOX, C_OUT), BF16),
            pltpu.VMEM((WSLOTS, C_OUT), F32),
            pltpu.VMEM((WSLOTS, C_OUT), F32),
            pltpu.VMEM((WSLOTS, C_OUT), F32),
            pltpu.VMEM((WSLOTS, C_OUT), F32),
            pltpu.VMEM((8, 128), F32),
            pltpu.VMEM((n_tile, 8, 128), F32),
            pltpu.VMEM((2, ROWS, 128), F32),
            pltpu.VMEM((ROWS, 128), F32),
            pltpu.VMEM((chips, share, 128), F32),
            pltpu.VMEM((SIDE, share, 128), F32),
            pltpu.VMEM((SIDE, share, 128), F32),
            pltpu.VMEM((padded, 128), F32),
            pltpu.VMEM((n_rep, padded // n_rep, 128), F32),
            pltpu.VMEM((2, padded, 128), F32),
            pltpu.VMEM((n_rep, 8, 128), F32),
            pltpu.VMEM((8, 128), F32),
            pltpu.VMEM((n_tile, 8, 128), F32),
        ]
        + [dma((n_tile,))] * 4
        + [dma((14,))] * 2
        + [dma((chips,))] * 2
        + [dma((SIDE,))] * 2
        + [dma((n_rep,))] * 2
        + [dma((2 * n_rep,))] * 2
        + [dma((n_rep,))] * 2
        + [
            pltpu.VMEM((n_tile, 1, 128), jnp.int32),
            pltpu.SMEM((n_tile, 1, 128), jnp.int32),
            pltpu.VMEM((PLANES, lines // RMOD + 1, 8 * WBLK, C_IN), BF16),
            pltpu.VMEM(((PLANES + 1) * depth, WBLK + 1, 8, C_IN), F32),
            pltpu.VMEM((PART * PIECE, C_IN), F32),
            pltpu.VMEM((n_tile * PARTS, PART * PIECE, C_IN), BF16),
            pltpu.VMEM((STOPS * PARTS, PART * PIECE, C_IN), BF16),
            pltpu.VMEM((STOPS * 2 * PART, 16, C_IN), F32),
            dma((n_tile,)),
            dma((n_tile,)),
            dma,
            dma((TH * FMOD,)),
            dma((lines // RMOD + 1,)),
            dma((TH,)),
            dma((n_tile * PARTS,)),
            dma((STOPS * PARTS,)),
        ],
        compiler_params=pltpu.CompilerParams(collective_id=0, has_side_effects=True, vmem_limit_bytes=VMEM_BYTES),
        cost_estimate=pl.CostEstimate(flops=4 * WSLOTS * VOX * ROWS * C_OUT, bytes_accessed=16 * 1024 * 1024, transcendentals=WSLOTS * VOX * C_OUT),
        name="conv_norm",
    )(strip, mine, meta, filt, up, clips, gains, shifts)


def shards(
    input_video,
    block_clip,
    send_slot,
    recv_index,
    tile_clip,
    kernel,
    norm_gain,
    norm_shift,
    upstream,
):
    peer_count = lax.axis_size("tile")
    me = lax.axis_index("tile")
    strip = input_video[0].reshape(PLANES, FMOD, TH, 8 * WBLK, C_IN)
    clip_ids = block_clip[0]
    mine = jnp.concatenate(
        [send_slot[0, 0].reshape(-1), recv_index[0, 0], jnp.zeros((128 - 2 * peer_count - WSLOTS,), jnp.int32)]
    )[None]
    depth = peer_count * TH // RMOD + 2
    block = jnp.arange(TBLK, dtype=jnp.int32)
    place = (me % FMOD - TT * block + 2) % FMOD
    linked = jnp.concatenate([jnp.zeros((1,), bool), clip_ids[1:] == clip_ids[:-1]])
    plane = jnp.where((place >= 2) | linked, (TT * block - 2 + place) // FMOD, PLANES)
    owner = jnp.arange(peer_count, dtype=jnp.int32)
    top = owner * TH - 1
    line = (top + (me // FMOD - top) % RMOD - me // FMOD + RMOD) // RMOD
    meta = jnp.concatenate(
        [plane * depth, jnp.zeros((2,), jnp.int32), line, jnp.zeros((120 - peer_count,), jnp.int32)]
    )[None]
    activation, grad_rows, norm_rows = main_call(
        peer_count, lax.axis_size("rep"), strip, mine, meta, kernel, upstream[0, 0],
        tile_clip[0, 0][:, None], norm_gain[None], norm_shift[None]
    )
    row_share = ROWS // peer_count
    skip = (grad_rows.shape[0] - row_share) * lax.rem(lax.axis_index("tile"), 2)
    grad_shard = lax.dynamic_slice_in_dim(grad_rows, skip, row_share, 0)
    return (activation[None, None], grad_shard, norm_rows[2:6].reshape(2, C_OUT))


def solution(mesh):
    placed = (
        P("rep", None, "tile", None, None),
        P("rep", None),
        P("rep", "tile", None, None),
        P("rep", "tile", None),
        P("rep", "tile", None),
        P(),
        P(),
        P(),
        P("rep", "tile", None, None, None),
    )
    return jax.shard_map(
        shards,
        mesh=mesh,
        in_specs=placed,
        out_specs=(P("rep", "tile", None, None, None), P("tile", None), P()),
        check_vma=False,
    )
```
